256 devices in a mesh: row: 4 (over x), col: 16 (over y_hi, z), seq: 4 (over y_lo, core).
Axes of the slice: x: 4, y: 4 (y_hi: 2, y_lo: 2; y = y_hi * 2 + y_lo), z: 8, core: 2. Of those that a mesh axis runs over, the one named last changes fastest.
Arguments:
- left: bfloat16 [128, 32, 768], P('seq', 'col', 'row'), may hold values from -6 to 6
- right: bfloat16 [128, 32, 768], P('seq', 'row', 'col'), may hold values from -6 to 6
- projection: bfloat16 [1024, 128], replicated, may hold values from -2 to 2
- bias: float32 [128], replicated, may hold values from -3 to 3
- cotangent: bfloat16 [768, 768, 128], P(('row', 'seq'), 'col'), may hold values from -1.1953125 to 1.1953125
Outputs:
- pair: bfloat16 [768, 768, 128], P(('row', 'seq'), 'col')
- left_grad: float32 [128, 32, 768], P('seq', 'col', 'row')
- right_grad: float32 [128, 32, 768], P('seq', 'row', 'col')
- weight_grad: float32 [1024, 128], replicated
The draws below stay inside these ranges and needn't reach their ends.
All inputs are finite; a program needn't handle non-finite values.
Results may differ from the reference program's by a relative error of at most 0.019.
Values may be sent and summed in bfloat16 or wider, within the bound.
A program may use at most 128 MiB of HBM per device.

```python
import jax
import jax.numpy as jnp
from jax import lax

C = 32
CP = 128
S = 128
R = 768
N_SEQ = 4


def levels(own_key, shape, shards, least, largest):
    level = 1.0
    for position, parts in shards:
        steps = jax.random.uniform(jax.random.fold_in(jax.random.fold_in(own_key, 6), position), (parts,), jnp.float32, least / len(shards), largest / len(shards))
        level = level * jnp.repeat(jnp.exp(steps), shape[position] // parts).reshape((-1,) + (1,) * (len(shape) - 1 - position))
    return level


def bell_draw(own_key, shape, spread, limit, split=(), held_as=jnp.bfloat16):
    array = jax.random.normal(own_key, shape, jnp.float32) * spread
    if len(split) > 0:
        array = levels(own_key, shape, split, -0.22, 0.18) * array
    return jnp.clip(array, min=-limit, max=limit).astype(held_as)


def setup_inputs(seed: int = 0) -> dict:
    seeds = jax.random.split(jax.random.key(seed), 6)
    return {
        "left": bell_draw(seeds[0], (S, C, R), 1.0, 6.0, ((0, 4), (1, 16), (2, 4))),
        "right": bell_draw(seeds[1], (S, C, R), 1.0, 6.0, ((0, 4), (1, 4), (2, 16))),
        "projection": bell_draw(seeds[2], (C * C, CP), (C * C // S) ** -0.5, 2.0),
        "bias": bell_draw(seeds[3], (CP,), 0.5, 3.0, (), jnp.float32),
        "cotangent": bell_draw(seeds[4], (R, R, CP), 0.2, 1.1953125, ((0, 16), (1, 16))),
    }


def reference(left, right, projection, bias, cotangent):
    groups = N_SEQ
    per = S // groups
    blk = 16
    while R % blk != 0:
        blk = blk // 2
    left_g = left.reshape(groups, per, C, R)
    right_g = right.reshape(groups, per, C, R)
    right_f = right.astype(jnp.float32)
    w_t = projection.T

    def step(carry, index):
        grad_w, grad_b = carry
        start = (index * blk).astype(jnp.int32)
        a_blk = lax.dynamic_slice_in_dim(left_g, start, blk, 3)
        dz_blk = lax.dynamic_slice_in_dim(cotangent, start, blk, 0)
        dz_flat = dz_blk.reshape(blk * R, CP)
        total = jnp.zeros((blk * R, CP), jnp.float32)
        for group in range(groups):
            outer = jnp.einsum("sci,sej->ijce", a_blk[group].astype(jnp.float32), right_g[group].astype(jnp.float32))
            outer = outer.reshape(blk * R, C * C).astype(jnp.bfloat16)
            part = jnp.dot(outer, projection, preferred_element_type=jnp.float32).astype(jnp.bfloat16)
            total = total + part.astype(jnp.float32)
            grad_w = grad_w + jnp.dot(outer.T, dz_flat, preferred_element_type=jnp.float32)
        pair_blk = (total / S + bias).astype(jnp.bfloat16).reshape(blk, R, CP)
        d_outer = (jnp.dot(dz_flat, w_t, preferred_element_type=jnp.float32) / S).astype(jnp.bfloat16)
        d_outer = d_outer.reshape(blk, R, C, C).astype(jnp.float32)
        grad_a = jnp.einsum("ijce,sej->sci", d_outer, right_f)
        a_all = a_blk.reshape(S, C, blk).astype(jnp.float32)
        grad_b = grad_b + jnp.einsum("ijce,sci->sej", d_outer, a_all)
        return (grad_w, grad_b), (pair_blk, grad_a)

    init = (jnp.zeros((C * C, CP), jnp.float32), jnp.zeros((S, C, R), jnp.float32))
    (grad_w, grad_b), (pairs, grads_a) = lax.scan(step, init, jnp.arange(R // blk, dtype=jnp.int32))
    pair = pairs.reshape(R, R, CP)
    left_grad = jnp.transpose(grads_a, (1, 2, 0, 3)).reshape(S, C, R)
    return pair, left_grad, grad_b, grad_w / S
```

```python
import functools

import jax
import jax.numpy as jnp
from jax import lax
from jax.experimental import pallas as pl
from jax.experimental.pallas import tpu as pltpu
from jax.sharding import PartitionSpec as P

MESH = pl.DeviceIdType.MESH
F32 = jnp.float32
BF16 = jnp.bfloat16
NZ = 8


def dot(a, b, dims):
    return lax.dot_general(a, b, (dims, ((), ())), preferred_element_type=F32)


NN = ((1,), (0,))
NT = ((1,), (1,))


def kernel(n, xl, xr, cot, w3, w2t, bias, pair, lg, rg, wg,
           l1, lp, ltf, lt, ltt, rbuf, rt, dbuf, obuf, cbd, gtf, gsend, grecv, hsend, hrecv,
           g2send, g2recv, wsend, wrecv, w1send, zrecv, w2send, wall, wacc, ssem, rsem):
    NR, NC, NS, NZ = n
    NYH = NC // NZ
    NA = NR * NS
    NP = NR * NYH * NS
    SB = xl.shape[1]
    I, J, CP = cot.shape
    JP = xl.shape[2] // 2
    NER = xr.shape[0]
    NE = NER * NR
    C = 2 * NC
    S = SB * NS
    IB = 8
    WR = (NE * C) // NP

    r = lax.axis_index("row")
    c = lax.axis_index("col")
    s = lax.axis_index("seq")
    z = lax.rem(c, NZ)
    yh = lax.div(c, NZ)
    ia = r * NS + s
    ip = (r * NYH + yh) * NS + s

    def seq_peer(k):
        return (r, c, lax.rem(s + k, NS))

    def row_seq_peer(k):
        t = lax.rem(ia + k, NA)
        return (lax.div(t, NS), c, lax.rem(t, NS))

    def col_peer(k):
        return (r, lax.rem(c + k, NC), s)

    def plane_index(k):
        return lax.rem(ip + k, NP)

    def plane_peer(k):
        t = plane_index(k)
        return (lax.div(t, NYH * NS), lax.rem(lax.div(t, NS), NYH) * NZ + z, lax.rem(t, NS))

    def z_peer(k):
        return (r, yh * NZ + lax.rem(z + k, NZ), s)

    def loop(lo, hi, f):
        def step(k, carry):
            f(k)
            return carry
        lax.fori_loop(lo, hi, step, 0)

    def send(src, dst, phase, dev):
        pltpu.make_async_remote_copy(
            src_ref=src, dst_ref=dst, send_sem=ssem.at[phase], recv_sem=rsem.at[phase],
            device_id=dev, device_id_type=MESH,
        ).start()

    def wait_recv(ref, phase):
        pltpu.make_async_copy(ref, ref, rsem.at[phase]).wait()

    def wait_send(ref, phase):
        pltpu.make_async_copy(ref, ref, ssem.at[phase]).wait()

    barrier = pltpu.get_barrier_semaphore()

    def greet(dev):
        pl.semaphore_signal(barrier, inc=1, device_id=dev, device_id_type=MESH)

    loop(1, NP, lambda k: greet(plane_peer(k)))
    loop(1, NZ, lambda k: greet(col_peer(k)))
    loop(NZ + 1, NC, lambda k: greet(col_peer(k)))
    pl.semaphore_wait(barrier, NP - 1 + NC - NYH)

    srow = pl.multiple_of(s * SB, SB)
    erow = pl.multiple_of(r * NER, NER)

    loop(1, NS, lambda k: send(xl.at[lax.rem(s + k, NS)], l1.at[pl.ds(srow, SB)], 0, seq_peer(k)))
    loop(1, NA, lambda k: send(xr, rbuf.at[pl.ds(erow, NER), pl.ds(srow, SB)], 1, row_seq_peer(k)))
    l1[pl.ds(srow, SB), :] = xl[s]
    rbuf[pl.ds(erow, NER), pl.ds(srow, SB), :] = xr[...]
    wait_recv(l1.at[pl.ds(0, (NS - 1) * SB)], 0)

    x = l1[...].astype(F32).T
    lp[c, pl.ds(0, I), :] = x[0:I].astype(BF16)
    lp[c, pl.ds(I, I), :] = x[JP:JP + I].astype(BF16)
    loop(1, NC, lambda k: send(lp.at[c], lp.at[c], 2, col_peer(k)))

    def d_step(k):
        zero = jnp.zeros((JP, CP), BF16)
        for q in range(2):
            i = 2 * k + q
            a = jnp.concatenate([cot[i], jnp.zeros((JP - J, CP), BF16)], axis=0)
            cbd[i, pl.ds(0, JP), :] = jnp.concatenate([a, zero], axis=1)
            cbd[i, pl.ds(JP, JP), :] = jnp.concatenate([zero, a], axis=1)
        rhs = cbd[pl.ds(2 * k, 2)].reshape(4 * JP, 2 * CP)
        d = dot(w3[...], rhs, NT).astype(BF16)
        dbuf[2 * k] = d[:, :2 * JP]
        dbuf[2 * k + 1] = d[:, 2 * JP:]

    loop(0, I // 2, d_step)

    wait_recv(rbuf.at[pl.ds(0, (NE * (NA - 1)) // NA)], 1)
    for e in range(NE):
        rt[pl.ds(e * 2 * JP, 2 * JP), :] = rbuf[e].astype(F32).T.astype(BF16)

    def g_step(k):
        base = k * IB
        lhs = jnp.concatenate(
            [dbuf[pl.ds(base, IB), pl.ds(e * C, C), :].reshape(IB * C, 2 * JP) for e in range(NE)], axis=1
        )
        gtf[pl.ds(pl.multiple_of(base * C, IB * C), IB * C), :] = dot(lhs, rt[...], NN)

    loop(0, I // IB, g_step)
    for q in range(NC):
        for h in range(2):
            gsend[q, pl.ds(h * I, I), :] = gtf[pl.ds(2 * q + h, I, stride=C), :].astype(BF16)
    loop(1, NC, lambda k: send(gsend.at[lax.rem(c + k, NC)], grecv.at[c], 3, col_peer(k)))
    grecv[c] = gsend[c]

    wait_recv(lp.at[pl.ds(0, NC - 1)], 2)
    for q in range(NC):
        for h in range(2):
            ltf[pl.ds(2 * q + h, I, stride=C), :] = lp[q, pl.ds(h * I, I), :].astype(F32)

    def o_step(k):
        base = k * IB
        rows = pl.ds(pl.multiple_of(base * C, IB * C), IB * C)
        a = ltf[rows, :].astype(BF16)
        lt[rows, :] = a
        rhs = jnp.concatenate([rbuf[e] for e in range(NE)], axis=1)
        o = dot(a, rhs, NN).astype(BF16)
        for e in range(NE):
            obuf[pl.ds(base, IB), pl.ds(e * C, C), :] = o[:, e * 2 * JP:(e + 1) * 2 * JP].reshape(IB, C, 2 * JP)

    loop(0, I // IB, o_step)
    wacc[...] = jnp.zeros_like(wacc)

    def w_step(k):
        base = k * IB
        lhs = jnp.concatenate([obuf[base + q] for q in range(IB)], axis=1)
        rhs = cbd[pl.ds(base, IB)].reshape(IB * 2 * JP, 2 * CP)
        wacc[...] += dot(lhs, rhs, NN)

    loop(0, I // IB, w_step)
    for q in range(NP):
        wsend[q] = wacc[pl.ds(q * WR, WR), :].astype(BF16)
    loop(1, NP, lambda k: send(wsend.at[plane_index(k)], wrecv.at[ip], 4, plane_peer(k)))
    wrecv[ip] = wsend[ip]

    for q in range((I * C) // S):
        ltt[:, pl.ds(q * S, S)] = ltf[pl.ds(q * S, S), :].T.astype(BF16)

    def h_step(k):
        rhs = jnp.concatenate(
            [dbuf[:, pl.ds(pl.multiple_of((2 * k + q) * C, C), C), :].reshape(I * C, 2 * JP) for q in range(2)],
            axis=1,
        )
        h = dot(ltt[...], rhs, NN).astype(BF16)
        hsend[2 * k] = h[:, :2 * JP]
        hsend[2 * k + 1] = h[:, 2 * JP:]

    loop(0, NE // 2, h_step)

    def h_piece(t):
        return hsend.at[
            pl.ds(pl.multiple_of(lax.div(t, NS) * NER, NER), NER),
            pl.ds(pl.multiple_of(lax.rem(t, NS) * SB, SB), SB),
        ]

    loop(1, NA, lambda k: send(h_piece(lax.rem(ia + k, NA)), hrecv.at[ia], 5, row_seq_peer(k)))
    hrecv[ia] = hsend[pl.ds(erow, NER), pl.ds(srow, SB), :]

    wait_recv(wrecv.at[pl.ds(0, NP - 1)], 4)
    total = wrecv[0].astype(F32)
    for q in range(1, NP):
        total = total + wrecv[q].astype(F32)
    w1send[...] = total.astype(BF16)
    loop(1, NZ, lambda k: send(w1send, zrecv.at[z], 6, z_peer(k)))
    zrecv[z] = w1send[...]

    def p_step(k):
        rhs = jnp.concatenate([obuf[2 * k], obuf[2 * k + 1]], axis=1)
        y = dot(w2t[...], rhs, NN)
        lo, hi = y[:CP], y[CP:]
        a = lo[:, :2 * JP] + pltpu.roll(hi[:, :2 * JP], JP, 1)
        b = hi[:, 2 * JP:] + pltpu.roll(lo[:, 2 * JP:], JP, 1)
        lane = lax.broadcasted_iota(jnp.int32, a.shape, 1)
        m = jnp.where(lane < JP, a, b).T * (1.0 / S) + bias[...]
        m = m.astype(BF16)
        pair[2 * k] = m[:J]
        pair[2 * k + 1] = m[JP:JP + J]

    loop(0, I // 4, p_step)

    wait_recv(zrecv.at[pl.ds(0, NZ - 1)], 6)
    total = zrecv[0].astype(F32)
    for q in range(1, NZ):
        total = total + zrecv[q].astype(F32)
    w2send[...] = (total * (1.0 / S)).astype(BF16)
    loop(1, NP, lambda k: send(w2send, wall.at[ip], 7, plane_peer(k)))
    wall[ip] = w2send[...]

    loop(I // 4, I // 2, p_step)

    wait_recv(grecv.at[pl.ds(0, NC - 1)], 3)
    total = grecv[0].astype(F32)
    for q in range(1, NC):
        total = total + grecv[q].astype(F32)
    pad = jnp.zeros((JP - I, S), F32)
    t = jnp.concatenate([total[:I], pad, total[I:], pad], axis=0) * (1.0 / S)
    g2send[...] = t.T.astype(BF16)
    loop(1, NS, lambda k: send(
        g2send.at[pl.ds(pl.multiple_of(lax.rem(s + k, NS) * SB, SB), SB)], g2recv.at[s], 8, seq_peer(k)))
    g2recv[s] = g2send[pl.ds(srow, SB), :]

    wait_recv(hrecv.at[pl.ds(0, NA - 1)], 5)
    for e in range(NER):
        total = hrecv[0, e].astype(F32)
        for q in range(1, NA):
            total = total + hrecv[q, e].astype(F32)
        rg[e] = total * (1.0 / S)

    wait_recv(wall.at[pl.ds(0, NP - 1)], 7)
    for q in range(NP):
        wg[pl.ds(q * WR, WR), :] = wall[q]

    wait_recv(g2recv.at[pl.ds(0, NS - 1)], 8)
    lg[...] = g2recv[...].astype(F32)

    wait_send(l1.at[pl.ds(0, (NS - 1) * SB)], 0)
    wait_send(rbuf.at[pl.ds(0, (NE * (NA - 1)) // NA)], 1)
    wait_send(lp.at[pl.ds(0, NC - 1)], 2)
    wait_send(grecv.at[pl.ds(0, NC - 1)], 3)
    wait_send(wrecv.at[pl.ds(0, NP - 1)], 4)
    wait_send(hrecv.at[pl.ds(0, NA - 1)], 5)
    wait_send(zrecv.at[pl.ds(0, NZ - 1)], 6)
    wait_send(wall.at[pl.ds(0, NP - 1)], 7)
    wait_send(g2recv.at[pl.ds(0, NS - 1)], 8)


def body(n, left, right, projection, bias, cotangent):
    NR, NC, NS, NZ = n
    NYH = NC // NZ
    NA = NR * NS
    NP = NR * NYH * NS
    SB = left.shape[0]
    S = SB * NS
    C = 2 * NC
    I, J, CP = cotangent.shape
    JP = -(-J // 64) * 64 if J >= 48 else 2 * J
    NER = right.shape[1] // 2
    NE = NER * NR
    WR = (NE * C) // NP

    xl = left.reshape(SB, 2, NS, I).transpose(2, 0, 1, 3)
    xl = jnp.pad(xl, ((0, 0), (0, 0), (0, 0), (0, JP - I))).reshape(NS, SB, 2 * JP)
    xr = right.reshape(SB, NER, 2, J).transpose(1, 0, 2, 3)
    xr = jnp.pad(xr, ((0, 0), (0, 0), (0, 0), (0, JP - J))).reshape(NER, SB, 2 * JP)
    w3 = projection.reshape(C, NE, 2, CP).transpose(1, 0, 2, 3).reshape(NE * C, 2 * CP)
    w2t = w3.T

    vmem = pl.BlockSpec(memory_space=pltpu.VMEM)
    scratch = [
        pltpu.VMEM((S, 2 * JP), BF16),
        pltpu.VMEM((NC, 2 * I, S), BF16),
        pltpu.VMEM((I * C, S), F32),
        pltpu.VMEM((I * C, S), BF16),
        pltpu.VMEM((S, I * C), BF16),
        pltpu.VMEM((NE, S, 2 * JP), BF16),
        pltpu.VMEM((NE * 2 * JP, S), BF16),
        pltpu.VMEM((I, NE * C, 2 * JP), BF16),
        pltpu.VMEM((I, NE * C, 2 * JP), BF16),
        pltpu.VMEM((I, 2 * JP, 2 * CP), BF16),
        pltpu.VMEM((I * C, S), F32),
        pltpu.VMEM((NC, 2 * I, S), BF16),
        pltpu.VMEM((NC, 2 * I, S), BF16),
        pltpu.VMEM((NE, S, 2 * JP), BF16),
        pltpu.VMEM((NA, NER, SB, 2 * JP), BF16),
        pltpu.VMEM((S, 2 * JP), BF16),
        pltpu.VMEM((NS, SB, 2 * JP), BF16),
        pltpu.VMEM((NP, WR, 2 * CP), BF16),
        pltpu.VMEM((NP, WR, 2 * CP), BF16),
        pltpu.VMEM((WR, 2 * CP), BF16),
        pltpu.VMEM((NZ, WR, 2 * CP), BF16),
        pltpu.VMEM((WR, 2 * CP), BF16),
        pltpu.VMEM((NP, WR, 2 * CP), BF16),
        pltpu.VMEM((NE * C, 2 * CP), F32),
        pltpu.SemaphoreType.DMA((9,)),
        pltpu.SemaphoreType.DMA((9,)),
    ]
    pair, lg, rg, wg = pl.pallas_call(
        functools.partial(kernel, n),
        out_shape=(
            jax.ShapeDtypeStruct((I, J, CP), BF16),
            jax.ShapeDtypeStruct((NS, SB, 2 * JP), F32),
            jax.ShapeDtypeStruct((NER, SB, 2 * JP), F32),
            jax.ShapeDtypeStruct((NE * C, 2 * CP), BF16),
        ),
        in_specs=[vmem] * 6,
        out_specs=(vmem,) * 4,
        scratch_shapes=scratch,
        compiler_params=pltpu.CompilerParams(
            collective_id=0, has_side_effects=True, vmem_limit_bytes=48 * 1024 * 1024
        ),
    )(xl, xr, cotangent, w3, w2t, bias.reshape(1, CP))

    left_grad = lg.reshape(NS, SB, 2, JP)[..., :I].transpose(1, 2, 0, 3).reshape(SB, 2, NS * I)
    right_grad = rg.reshape(NER, SB, 2, JP)[..., :J].transpose(1, 0, 2, 3).reshape(SB, 2 * NER, J)
    weight_grad = wg.reshape(NE, C, 2, CP).transpose(1, 0, 2, 3).reshape(NE * C * 2, CP).astype(F32)
    return pair, left_grad, right_grad, weight_grad


def solution(mesh, nz=NZ):
    n = (mesh.shape["row"], mesh.shape["col"], mesh.shape["seq"], nz)
    return jax.shard_map(
        functools.partial(body, n),
        mesh=mesh,
        in_specs=(
            P("seq", "col", "row"),
            P("seq", "row", "col"),
            P(),
            P(),
            P(("row", "seq"), "col", None),
        ),
        out_specs=(
            P(("row", "seq"), "col", None),
            P("seq", "col", "row"),
            P("seq", "row", "col"),
            P(),
        ),
        check_vma=False,
    )
```

```python
import functools

import jax
import jax.numpy as jnp
from jax import lax
from jax.experimental import pallas as pl
from jax.experimental.pallas import tpu as pltpu
from jax.sharding import PartitionSpec as P

MESH = pl.DeviceIdType.MESH
F32 = jnp.float32
BF16 = jnp.bfloat16
NZ = 8


def dot(a, b, dims):
    return lax.dot_general(a, b, (dims, ((), ())), preferred_element_type=F32)


NN = ((1,), (0,))
NT = ((1,), (1,))


def kernel(n, left, right, cot_in, w_in, bias, pair_out, lg, rg, wg,
           leftv, rightv, rightf, cot, wv, wf, w3, w2t, xl, xr,
           lbuf, ltf, ltt, rbuf, rt, dbuf, obuf, cbd, gtf, gsend, grecv, hsend, hrecv,
           g2send, g2recv, wsend, wrecv, w1send, zrecv, w2send, wall, wacc, pair, ssem, rsem, lsem):
    NR, NC, NS, NZ = n
    NYH = NC // NZ
    NA = NR * NS
    NP = NR * NYH * NS
    NL = NC * NS
    SB = xl.shape[1]
    I, J, CP = cot.shape
    JP = xl.shape[2] // 2
    L2 = 2 * JP
    NER = xr.shape[0]
    NE = NER * NR
    C = 2 * NC
    CH = C // 2
    S = SB * NS
    IB = 16

    r = lax.axis_index("row")
    c = lax.axis_index("col")
    s = lax.axis_index("seq")
    z = c % NZ
    yh = c // NZ
    ia = r * NS + s
    ip = (r * NYH + yh) * NS + s
    il = c * NS + s

    def seq_peer(k):
        return (r, c, (s + k) % NS)

    def row_seq_peer(k):
        t = (ia + k) % NA
        return (t // NS, c, t % NS)

    def col_peer(k):
        return (r, (c + k) % NC, s)

    def plane_device(t):
        return (t // (NYH * NS), ((t // NS) % NYH) * NZ + z, t % NS)

    def plane_peer(k):
        return plane_device((ip + k) % NP)

    def z_peer(k):
        return (r, yh * NZ + (z + k) % NZ, s)

    def loop(lo, hi, f):
        def step(k, carry):
            f(k)
            return carry
        lax.fori_loop(lo, hi, step, 0)

    def send(src, dst, phase, dev):
        pltpu.make_async_remote_copy(
            src_ref=src, dst_ref=dst, send_sem=ssem.at[phase], recv_sem=rsem.at[phase],
            device_id=dev, device_id_type=MESH,
        ).start()

    def wait_recv(ref, phase):
        pltpu.make_async_copy(ref, ref, rsem.at[phase]).wait()

    def wait_send(ref, phase):
        pltpu.make_async_copy(ref, ref, ssem.at[phase]).wait()

    loads = [
        pltpu.make_async_copy(src, dst, lsem.at[q])
        for q, (src, dst) in enumerate([(left, leftv), (right, rightv), (w_in, wv), (cot_in, cot)])
    ]
    for load in loads:
        load.start()

    barrier = pltpu.get_barrier_semaphore()

    def greet(dev):
        pl.semaphore_signal(barrier, inc=1, device_id=dev, device_id_type=MESH)

    def greet_row(k):
        t = (il + k) % NL
        greet((r, t // NS, t % NS))

    def greet_plane(k):
        t = (yh * NS + s + k) % (NYH * NS)
        q = k // (NYH * NS)
        greet(((r + q) % NR, (t // NS) * NZ + z, t % NS))

    loop(1, NL, greet_row)
    loop(NYH * NS, NP, greet_plane)

    loads[0].wait()
    loads[1].wait()
    lf = leftv[...].astype(F32)
    zero = jnp.zeros((SB, JP - I), F32)
    for q in range(NS):
        parts = []
        for h in range(2):
            parts += [lf[:, h, q * I:(q + 1) * I], zero]
        xl[q] = jnp.concatenate(parts, axis=1).astype(BF16)
    rightf[:, pl.ds(0, J)] = rightv[...].astype(F32).reshape(SB * 2 * NER, J)
    for e in range(NER):
        parts = []
        for h in range(2):
            parts += [rightf[pl.ds(2 * e + h, SB, stride=2 * NER), :][:, :J], zero]
        xr[e] = jnp.concatenate(parts, axis=1).astype(BF16)

    srow = pl.multiple_of(s * SB, SB)
    erow = pl.multiple_of(r * NER, NER)

    pl.semaphore_wait(barrier, NL - 1 + NP - NYH * NS)

    def send_left(half, k, phase):
        t = (z * NS + s + k) % (NZ * NS)
        send(xl.at[t % NS], lbuf.at[c, pl.ds(srow, SB)], phase, (r, half * NZ + t // NS, t % NS))

    loop(1, NZ * NS, lambda k: send_left(yh, k, 0))
    loop(1, NA, lambda k: send(xr, rbuf.at[pl.ds(erow, NER), pl.ds(srow, SB)], 1, row_seq_peer(k)))
    loop(0, NZ * NS, lambda k: send_left(1 - yh, k, 2))
    lbuf[c, pl.ds(srow, SB), :] = xl[s]
    rbuf[pl.ds(erow, NER), pl.ds(srow, SB), :] = xr[...]

    loads[2].wait()
    loads[3].wait()
    wf[...] = wv[...].astype(F32)
    for ah in range(2):
        for e in range(NE):
            for h in range(2):
                w3[pl.ds((ah * NE + e) * CH, CH), pl.ds(h * CP, CP)] = (
                    wf[pl.ds(ah * CH * 2 * NE + 2 * e + h, CH, stride=2 * NE), :].astype(BF16)
                )
    w2t[...] = w3[...].astype(F32).T.astype(BF16)

    def d_step(k):
        zc = jnp.zeros((JP, CP), BF16)
        for q in range(2):
            i = 2 * k + q
            a = jnp.concatenate([cot[i], jnp.zeros((JP - J, CP), BF16)], axis=0)
            cbd[i, pl.ds(0, JP), :] = jnp.concatenate([a, zc], axis=1)
            cbd[i, pl.ds(JP, JP), :] = jnp.concatenate([zc, a], axis=1)
        rhs = cbd[pl.ds(2 * k, 2)].reshape(2 * L2, 2 * CP)
        d = dot(w3[...], rhs, NT).astype(BF16)
        dbuf[2 * k] = d[:, :L2].reshape(2, NE, CH, L2)
        dbuf[2 * k + 1] = d[:, L2:].reshape(2, NE, CH, L2)

    loop(0, I // 2, d_step)

    wait_recv(rbuf.at[pl.ds(0, (NE * (NA - 1)) // NA)], 1)
    for e in range(NE):
        rt[pl.ds(e * L2, L2), :] = rbuf[e].astype(F32).T.astype(BF16)

    def g_step(k):
        base = k * 8
        lhs = jnp.concatenate(
            [dbuf[pl.ds(base, 8), :, e].reshape(8 * C, L2) for e in range(NE)], axis=1
        )
        gtf[pl.ds(pl.multiple_of(base * C, 8 * C), 8 * C), :] = dot(lhs, rt[...], NN)

    loop(0, I // 8, g_step)
    for q in range(NC):
        for h in range(2):
            gsend[q, pl.ds(h * I, I), :] = gtf[pl.ds(2 * q + h, I, stride=C), :].astype(BF16)

    def half_step(ah):
        lh = ltf.at[ah]
        for q in range(NZ):
            x = lbuf[ah * NZ + q].astype(F32).T
            for h in range(2):
                lh[pl.ds(2 * q + h, I, stride=CH), :] = x[h * JP:h * JP + I]

        def o_step(k):
            base = k * IB
            a = lh[pl.ds(pl.multiple_of(base * CH, IB * CH), IB * CH), :].astype(BF16)
            rhs = jnp.concatenate([rbuf[e] for e in range(NE)], axis=1)
            o = dot(a, rhs, NN).astype(BF16)
            for e in range(NE):
                obuf[pl.ds(base, IB), ah, e] = o[:, e * L2:(e + 1) * L2].reshape(IB, CH, L2)

        loop(0, I // IB, o_step)
        wacc[...] = jnp.zeros_like(wacc)

        def w_step(k):
            base = k * 8
            lhs = jnp.concatenate([obuf[base + q, ah].reshape(NE * CH, L2) for q in range(8)], axis=1)
            wacc[...] += dot(lhs, cbd[pl.ds(base, 8)].reshape(8 * L2, 2 * CP), NN)

        loop(0, I // 8, w_step)
        for e in range(NE):
            wsend[2 * e + ah] = wacc[pl.ds(e * CH, CH), :].astype(BF16)

        def send_piece(k):
            t = 2 * ((ip // 2 + k) % NE) + ah

            @pl.when(t != ip)
            def _():
                send(wsend.at[t], wrecv.at[ip], 4, plane_device(t))

        loop(0, NE, send_piece)

    wait_recv(gtf.at[pl.ds(0, (NZ * NS - 1) * SB // 2)], 0)
    half_step(yh)
    wait_recv(lbuf.at[pl.ds(0, NZ)], 2)
    half_step(1 - yh)
    wrecv[ip] = wsend[ip]
    loop(1, NC, lambda k: send(gsend.at[(c + k) % NC], grecv.at[c], 3, col_peer(k)))
    grecv[c] = gsend[c]

    for ah in range(2):
        for q in range((I * CH) // S):
            ltt[:, pl.ds((ah * I * CH) + q * S, S)] = ltf[ah, pl.ds(q * S, S), :].T.astype(BF16)

    def h_step(k):
        rhs = jnp.concatenate(
            [
                jnp.concatenate([dbuf[:, ah, 2 * k + q].reshape(I * CH, L2) for ah in range(2)], axis=0)
                for q in range(2)
            ],
            axis=1,
        )
        h = dot(ltt[...], rhs, NN).astype(BF16)
        hsend[2 * k] = h[:, :L2]
        hsend[2 * k + 1] = h[:, L2:]

    loop(0, NE // 2, h_step)

    wait_recv(wrecv.at[pl.ds(0, NP - 1)], 4)
    total = wrecv[0].astype(F32)
    for q in range(1, NP):
        total = total + wrecv[q].astype(F32)
    w1send[...] = total.astype(BF16)
    loop(1, NZ, lambda k: send(w1send, zrecv.at[z], 6, z_peer(k)))
    zrecv[z] = w1send[...]

    def h_piece(t):
        return hsend.at[
            pl.ds(pl.multiple_of((t // NS) * NER, NER), NER),
            pl.ds(pl.multiple_of((t % NS) * SB, SB), SB),
        ]

    loop(1, NA, lambda k: send(h_piece((ia + k) % NA), hrecv.at[ia], 5, row_seq_peer(k)))
    hrecv[ia] = hsend[pl.ds(erow, NER), pl.ds(srow, SB), :]

    def p_step(k):
        rhs = jnp.concatenate(
            [obuf[2 * k].reshape(NE * C, L2), obuf[2 * k + 1].reshape(NE * C, L2)], axis=1
        )
        y = dot(w2t[...], rhs, NN)
        lo, hi = y[:CP], y[CP:]
        a = lo[:, :L2] + pltpu.roll(hi[:, :L2], JP, 1)
        b = hi[:, L2:] + pltpu.roll(lo[:, L2:], JP, 1)
        lane = lax.broadcasted_iota(jnp.int32, a.shape, 1)
        m = jnp.where(lane < JP, a, b).T * (1.0 / S) + bias[...]
        m = m.astype(BF16)
        pair[2 * k] = m[:J]
        pair[2 * k + 1] = m[JP:JP + J]

    loop(0, I // 4, p_step)

    wait_recv(zrecv.at[pl.ds(0, NZ - 1)], 6)
    total = zrecv[0].astype(F32)
    for q in range(1, NZ):
        total = total + zrecv[q].astype(F32)
    w2send[...] = (total * (1.0 / S)).astype(BF16)
    loop(1, NP, lambda k: send(w2send, wall.at[ip], 7, plane_peer(k)))
    wall[ip] = w2send[...]

    loop(I // 4, I // 2, p_step)
    store = pltpu.make_async_copy(pair, pair_out, lsem.at[4])
    store.start()

    wait_recv(grecv.at[pl.ds(0, NC - 1)], 3)
    total = grecv[0].astype(F32)
    for q in range(1, NC):
        total = total + grecv[q].astype(F32)
    pad = jnp.zeros((JP - I, S), F32)
    t = jnp.concatenate([total[:I], pad, total[I:], pad], axis=0) * (1.0 / S)
    g2send[...] = t.T.astype(BF16)
    loop(1, NS, lambda k: send(
        g2send.at[pl.ds(pl.multiple_of(((s + k) % NS) * SB, SB), SB)], g2recv.at[s], 8, seq_peer(k)))
    g2recv[s] = g2send[pl.ds(srow, SB), :]

    wait_recv(hrecv.at[pl.ds(0, NA - 1)], 5)
    for e in range(NER):
        total = hrecv[0, e].astype(F32)
        for q in range(1, NA):
            total = total + hrecv[q, e].astype(F32)
        total = total * (1.0 / S)
        for h in range(2):
            rg[:, 2 * e + h, :] = total[:, h * JP:h * JP + J]

    wait_recv(g2recv.at[pl.ds(0, NS - 1)], 8)
    for h in range(2):
        lg[:, h, :] = jnp.concatenate(
            [g2recv[q].astype(F32)[:, h * JP:h * JP + I] for q in range(NS)], axis=1
        )

    wait_recv(wall.at[pl.ds(0, NP - 1)], 7)
    for ah in range(2):
        for e in range(NE):
            x = wall[2 * e + ah].astype(F32)
            for h in range(2):
                wg[pl.ds(ah * CH * 2 * NE + 2 * e + h, CH, stride=2 * NE), :] = x[:, h * CP:(h + 1) * CP]

    wait_send(gtf.at[pl.ds(0, (NZ * NS - 1) * SB // 2)], 0)
    wait_send(rbuf.at[pl.ds(0, (NE * (NA - 1)) // NA)], 1)
    wait_send(lbuf.at[pl.ds(0, NZ)], 2)
    wait_send(grecv.at[pl.ds(0, NC - 1)], 3)
    wait_send(wrecv.at[pl.ds(0, NP - 1)], 4)
    wait_send(hrecv.at[pl.ds(0, NA - 1)], 5)
    wait_send(zrecv.at[pl.ds(0, NZ - 1)], 6)
    wait_send(wall.at[pl.ds(0, NP - 1)], 7)
    wait_send(g2recv.at[pl.ds(0, NS - 1)], 8)
    store.wait()


def body(n, left, right, projection, bias, cotangent):
    NR, NC, NS, NZ = n
    NYH = NC // NZ
    NA = NR * NS
    NP = NR * NYH * NS
    SB = left.shape[0]
    S = SB * NS
    C = 2 * NC
    CH = C // 2
    I, J, CP = cotangent.shape
    JP = 64 if J == 48 else 2 * J
    L2 = 2 * JP
    NER = right.shape[1] // 2
    NE = NER * NR

    vmem = pl.BlockSpec(memory_space=pltpu.VMEM)
    hbm = pl.BlockSpec(memory_space=pl.ANY)
    scratch = [
        pltpu.VMEM(left.shape, BF16),
        pltpu.VMEM(right.shape, BF16),
        pltpu.VMEM((SB * 2 * NER, 128), F32),
        pltpu.VMEM(cotangent.shape, BF16),
        pltpu.VMEM(projection.shape, BF16),
        pltpu.VMEM(projection.shape, F32),
        pltpu.VMEM((NE * C, 2 * CP), BF16),
        pltpu.VMEM((2 * CP, NE * C), BF16),
        pltpu.VMEM((NS, SB, L2), BF16),
        pltpu.VMEM((NER, SB, L2), BF16),
        pltpu.VMEM((NC, S, L2), BF16),
        pltpu.VMEM((2, I * CH, S), F32),
        pltpu.VMEM((S, I * C), BF16),
        pltpu.VMEM((NE, S, L2), BF16),
        pltpu.VMEM((NE * L2, S), BF16),
        pltpu.VMEM((I, 2, NE, CH, L2), BF16),
        pltpu.VMEM((I, 2, NE, CH, L2), BF16),
        pltpu.VMEM((I, L2, 2 * CP), BF16),
        pltpu.VMEM((I * C, S), F32),
        pltpu.VMEM((NC, 2 * I, S), BF16),
        pltpu.VMEM((NC, 2 * I, S), BF16),
        pltpu.VMEM((NE, S, L2), BF16),
        pltpu.VMEM((NA, NER, SB, L2), BF16),
        pltpu.VMEM((S, L2), BF16),
        pltpu.VMEM((NS, SB, L2), BF16),
        pltpu.VMEM((NP, CH, 2 * CP), BF16),
        pltpu.VMEM((NP, CH, 2 * CP), BF16),
        pltpu.VMEM((CH, 2 * CP), BF16),
        pltpu.VMEM((NZ, CH, 2 * CP), BF16),
        pltpu.VMEM((CH, 2 * CP), BF16),
        pltpu.VMEM((NP, CH, 2 * CP), BF16),
        pltpu.VMEM((NE * CH, 2 * CP), F32),
        pltpu.VMEM((I, J, CP), BF16),
        pltpu.SemaphoreType.DMA((9,)),
        pltpu.SemaphoreType.DMA((9,)),
        pltpu.SemaphoreType.DMA((5,)),
    ]
    return pl.pallas_call(
        functools.partial(kernel, n),
        out_shape=(
            jax.ShapeDtypeStruct((I, J, CP), BF16),
            jax.ShapeDtypeStruct(left.shape, F32),
            jax.ShapeDtypeStruct(right.shape, F32),
            jax.ShapeDtypeStruct(projection.shape, F32),
        ),
        in_specs=[hbm] * 4 + [vmem],
        out_specs=(hbm, vmem, vmem, vmem),
        scratch_shapes=scratch,
        compiler_params=pltpu.CompilerParams(
            collective_id=0, has_side_effects=True, vmem_limit_bytes=60 * 1024 * 1024
        ),
    )(left, right, cotangent, projection, bias.reshape(1, CP))


def solution(mesh, nz=NZ):
    n = (mesh.shape["row"], mesh.shape["col"], mesh.shape["seq"], nz)
    return jax.shard_map(
        functools.partial(body, n),
        mesh=mesh,
        in_specs=(
            P("seq", "col", "row"),
            P("seq", "row", "col"),
            P(),
            P(),
            P(("row", "seq"), "col", None),
        ),
        out_specs=(
            P(("row", "seq"), "col", None),
            P("seq", "col", "row"),
            P("seq", "row", "col"),
            P(),
        ),
        check_vma=False,
    )
```

```python
import functools
import math

import jax
import jax.numpy as jnp
from jax import lax
from jax.experimental import pallas as pl
from jax.experimental.pallas import tpu as pltpu
from jax.sharding import PartitionSpec as P

MESH = pl.DeviceIdType.MESH
F32 = jnp.float32
BF16 = jnp.bfloat16
NZ = 8


def dot(a, b, dims):
    return lax.dot_general(a, b, (dims, ((), ())), preferred_element_type=F32)


def log2(size):
    return size.bit_length() - 1


NN = ((1,), (0,))
NT = ((1,), (1,))


def kernel(n, left, right, cot_in, w_in, bias, pair, lg, rg, wg,
           leftv, rightv, rightf, cot, wv, wf, w3, w2t, xl, xr,
           lbuf, ltf, ltt, rbuf, rt, dbuf, obuf, cbd, gtf, gsend, grecv, hsend, hrecv,
           g2send, g2recv, wsend, wrecv, w1send, zrecv, w2send, wall, wacc, ssem, rsem, lsem):
    NR, NC, NS, NZ = n
    NYH = NC // NZ
    NA = NR * NS
    NP = NR * NYH * NS
    SB = xl.shape[1]
    I, J, CP = cot.shape
    JP = xl.shape[2] // 2
    L2 = 2 * JP
    NER = xr.shape[0]
    NE = NER * NR
    C = 2 * NC
    CH = C // 2
    S = SB * NS
    IB = I

    r = lax.axis_index("row")
    c = lax.axis_index("col")
    s = lax.axis_index("seq")
    z = c & (NZ - 1)
    yh = c // NZ
    ia = r * NS + s
    ip = (r * NYH + yh) * NS + s

    def seq_peer(k):
        return (r, c, (s + k) & (NS - 1))

    def row_seq_peer(k):
        t = (ia + k) & (NA - 1)
        return (t >> log2(NS), c, t & (NS - 1))

    def col_peer(k):
        return (r, (c + k) & (NC - 1), s)

    def plane_device(t):
        return (t >> log2(NYH * NS), ((t >> log2(NS)) & (NYH - 1)) * NZ + z, t & (NS - 1))

    def plane_peer(k):
        return plane_device((ip + k) & (NP - 1))

    def z_peer(k):
        return (r, yh * NZ + ((z + k) & (NZ - 1)), s)

    def loop(lo, hi, f, unroll=1):
        unroll = math.gcd(hi - lo, unroll)

        def step(k, carry):
            for q in range(unroll):
                f(lo + k * unroll + q)
            return carry
        lax.fori_loop(0, (hi - lo) // unroll, step, 0)

    def send(src, dst, phase, dev):
        pltpu.make_async_remote_copy(
            src_ref=src, dst_ref=dst, send_sem=ssem.at[phase], recv_sem=rsem.at[phase],
            device_id=dev, device_id_type=MESH,
        ).start()

    def wait_recv(ref, phase):
        pltpu.make_async_copy(ref, ref, rsem.at[phase]).wait()

    def wait_send(ref, phase):
        pltpu.make_async_copy(ref, ref, ssem.at[phase]).wait()

    loads = [
        pltpu.make_async_copy(src, dst, lsem.at[q])
        for q, (src, dst) in enumerate([(left, leftv), (right, rightv), (w_in, wv), (cot_in, cot)])
    ]
    for load in loads:
        load.start()

    barrier = pltpu.get_barrier_semaphore()

    def greet(dev):
        pl.semaphore_signal(barrier, inc=1, device_id=dev, device_id_type=MESH)

    def greet_col(k):
        for t in range(NS):
            greet((r, (c + k) & (NC - 1), t))

    def greet_row(k):
        for h in range(NYH):
            for t in range(NS):
                greet(((r + k) & (NR - 1), h * NZ + z, t))

    loop(1, NR, greet_row)
    loop(1, NC, greet_col)
    for k in range(1, NS):
        greet(seq_peer(k))

    loads[0].wait()
    loads[1].wait()
    lf = leftv[...].astype(F32)
    zero = jnp.zeros((SB, JP - I), F32)
    for q in range(NS):
        parts = []
        for h in range(2):
            parts += [lf[:, h, q * I:(q + 1) * I], zero]
        xl[q] = jnp.concatenate(parts, axis=1).astype(BF16)
    rightf[:, pl.ds(0, J)] = rightv[...].astype(F32).reshape(SB * 2 * NER, J)
    for e in range(NER):
        parts = []
        for h in range(2):
            parts += [rightf[pl.ds(2 * e + h, SB, stride=2 * NER), :][:, :J], zero]
        xr[e] = jnp.concatenate(parts, axis=1).astype(BF16)

    srow = pl.multiple_of(s * SB, SB)
    erow = pl.multiple_of(r * NER, NER)

    pl.semaphore_wait(barrier, NC * NS - 1 + NP - NYH * NS)

    def send_left(half, k, phase):
        for t in range(NS):
            send(xl.at[t], lbuf.at[c, pl.ds(srow, SB)], phase, (r, half * NZ + ((z + k) & (NZ - 1)), t))

    def send_right(k):
        for t in range(NS):
            send(xr, rbuf.at[pl.ds(erow, NER), pl.ds(srow, SB)], 1, ((r + k) & (NR - 1), c, t))

    loop(1, NR, send_right)
    for k in range(1, NS):
        send(xr, rbuf.at[pl.ds(erow, NER), pl.ds(srow, SB)], 1, seq_peer(k))
    for k in range(1, NS):
        send(xl.at[(s + k) & (NS - 1)], lbuf.at[c, pl.ds(srow, SB)], 0, seq_peer(k))
    loop(1, NZ, lambda k: send_left(yh, k, 0))
    loop(0, NZ, lambda k: send_left(1 - yh, k, 2))
    lbuf[c, pl.ds(srow, SB), :] = xl[s]
    rbuf[pl.ds(erow, NER), pl.ds(srow, SB), :] = xr[...]

    loads[2].wait()
    loads[3].wait()
    wf[...] = wv[...].astype(F32)
    for ah in range(2):
        for e in range(NE):
            for h in range(2):
                w3[pl.ds((ah * NE + e) * CH, CH), pl.ds(h * CP, CP)] = (
                    wf[pl.ds(ah * CH * 2 * NE + 2 * e + h, CH, stride=2 * NE), :].astype(BF16)
                )
    w2t[...] = w3[...].astype(F32).T.astype(BF16)

    def d_step(k):
        zc = jnp.zeros((JP, CP), BF16)
        for q in range(2):
            i = 2 * k + q
            a = jnp.concatenate([cot[i], jnp.zeros((JP - J, CP), BF16)], axis=0)
            cbd[i, pl.ds(0, JP), :] = jnp.concatenate([a, zc], axis=1)
            cbd[i, pl.ds(JP, JP), :] = jnp.concatenate([zc, a], axis=1)
        rhs = cbd[pl.ds(2 * k, 2)].reshape(2 * L2, 2 * CP)
        d = dot(w3[...], rhs, NT).astype(BF16)
        dbuf[2 * k] = d[:, :L2].reshape(2, NE, CH, L2)
        dbuf[2 * k + 1] = d[:, L2:].reshape(2, NE, CH, L2)

    loop(0, I // 2, d_step, 4)

    wait_recv(rbuf.at[pl.ds(0, (NE * (NA - 1)) // NA)], 1)
    for e in range(NE):
        rt[pl.ds(e * L2, L2), :] = rbuf[e].astype(F32).T.astype(BF16)

    def g_step(k):
        base = k * 8
        lhs = jnp.concatenate(
            [dbuf[pl.ds(base, 8), :, e].reshape(8 * C, L2) for e in range(NE)], axis=1
        )
        gtf[pl.ds(pl.multiple_of(base * C, 8 * C), 8 * C), :] = dot(lhs, rt[...], NN)

    loop(0, I // 8, g_step, 3)
    for q in range(NC):
        for h in range(2):
            gsend[q, pl.ds(h * I, I), :] = gtf[pl.ds(2 * q + h, I, stride=C), :].astype(BF16)

    def half_step(ah):
        lh = ltf.at[ah]
        for q in range(NZ):
            x = lbuf[ah * NZ + q].astype(F32).T
            for h in range(2):
                lh[pl.ds(2 * q + h, I, stride=CH), :] = x[h * JP:h * JP + I]

        def o_step(k):
            base = k * IB
            a = lh[pl.ds(pl.multiple_of(base * CH, IB * CH), IB * CH), :].astype(BF16)
            rhs = jnp.concatenate([rbuf[e] for e in range(NE)], axis=1)
            o = dot(a, rhs, NN).astype(BF16)
            for e in range(NE):
                obuf[pl.ds(base, IB), ah, e] = o[:, e * L2:(e + 1) * L2].reshape(IB, CH, L2)

        loop(0, I // IB, o_step)
        wacc[...] = jnp.zeros_like(wacc)

        def w_step(k):
            base = k * 8
            lhs = jnp.concatenate([obuf[base + q, ah].reshape(NE * CH, L2) for q in range(8)], axis=1)
            wacc[...] += dot(lhs, cbd[pl.ds(base, 8)].reshape(8 * L2, 2 * CP), NN)

        loop(0, I // 8, w_step, 3)
        for e in range(NE):
            wsend[2 * e + ah] = wacc[pl.ds(e * CH, CH), :].astype(BF16)

        def send_piece(k):
            t = 2 * (((ip >> 1) + k) & (NE - 1)) + ah

            @pl.when(t != ip)
            def _():
                send(wsend.at[t], wrecv.at[ip], 4, plane_device(t))

        loop(0, NE, send_piece)

    wait_recv(gtf.at[pl.ds(0, (NZ * NS - 1) * SB // 2)], 0)
    half_step(yh)
    wait_recv(lbuf.at[pl.ds(0, NZ)], 2)
    loop(1, NC, lambda k: send(gsend.at[(c + k) & (NC - 1)], grecv.at[c], 3, col_peer(k)))
    half_step(1 - yh)
    wrecv[ip] = wsend[ip]
    grecv[c] = gsend[c]

    for ah in range(2):
        for q in range((I * CH) // S):
            ltt[:, pl.ds((ah * I * CH) + q * S, S)] = ltf[ah, pl.ds(q * S, S), :].T.astype(BF16)

    def h_step(k):
        rhs = jnp.concatenate(
            [
                jnp.concatenate([dbuf[:, ah, 2 * k + q].reshape(I * CH, L2) for ah in range(2)], axis=0)
                for q in range(2)
            ],
            axis=1,
        )
        h = dot(ltt[...], rhs, NN).astype(BF16)
        hsend[2 * k] = h[:, :L2]
        hsend[2 * k + 1] = h[:, L2:]

    loop(0, NE // 2, h_step, 2)

    wait_recv(wrecv.at[pl.ds(0, NP - 1)], 4)
    total = wrecv[0].astype(F32)
    for q in range(1, NP):
        total = total + wrecv[q].astype(F32)
    w1send[...] = total.astype(BF16)
    loop(1, NZ, lambda k: send(w1send, zrecv.at[z], 6, z_peer(k)))
    zrecv[z] = w1send[...]

    def h_piece(t):
        return hsend.at[
            pl.ds(pl.multiple_of((t >> log2(NS)) * NER, NER), NER),
            pl.ds(pl.multiple_of((t & (NS - 1)) * SB, SB), SB),
        ]

    loop(1, NA, lambda k: send(h_piece((ia + k) & (NA - 1)), hrecv.at[ia], 5, row_seq_peer(k)))
    hrecv[ia] = hsend[pl.ds(erow, NER), pl.ds(srow, SB), :]

    def p_step(k):
        rhs = jnp.concatenate(
            [obuf[2 * k].reshape(NE * C, L2), obuf[2 * k + 1].reshape(NE * C, L2)], axis=1
        )
        y = dot(w2t[...], rhs, NN)
        lo, hi = y[:CP], y[CP:]
        a = lo[:, :L2] + pltpu.roll(hi[:, :L2], JP, 1)
        b = hi[:, L2:] + pltpu.roll(lo[:, L2:], JP, 1)
        lane = lax.broadcasted_iota(jnp.int32, a.shape, 1)
        m = jnp.where(lane < JP, a, b).T * (1.0 / S) + bias[...]
        m = m.astype(BF16)
        pair[2 * k] = m[:J]
        pair[2 * k + 1] = m[JP:JP + J]

    loop(0, I // 4, p_step, 4)

    wait_recv(zrecv.at[pl.ds(0, NZ - 1)], 6)
    total = zrecv[0].astype(F32)
    for q in range(1, NZ):
        total = total + zrecv[q].astype(F32)
    w2send[...] = (total * (1.0 / S)).astype(BF16)
    loop(1, NP, lambda k: send(w2send, wall.at[ip], 7, plane_peer(k)))
    wall[ip] = w2send[...]

    wait_recv(grecv.at[pl.ds(0, NC - 1)], 3)
    total = grecv[0].astype(F32)
    for q in range(1, NC):
        total = total + grecv[q].astype(F32)
    pad = jnp.zeros((JP - I, S), F32)
    t = jnp.concatenate([total[:I], pad, total[I:], pad], axis=0) * (1.0 / S)
    g2send[...] = t.T.astype(BF16)
    loop(1, NS, lambda k: send(
        g2send.at[pl.ds(pl.multiple_of(((s + k) & (NS - 1)) * SB, SB), SB)], g2recv.at[s], 8, seq_peer(k)))
    g2recv[s] = g2send[pl.ds(srow, SB), :]

    loop(I // 4, I // 2, p_step, 4)

    wait_recv(hrecv.at[pl.ds(0, NA - 1)], 5)
    for e in range(NER):
        total = hrecv[0, e].astype(F32)
        for q in range(1, NA):
            total = total + hrecv[q, e].astype(F32)
        total = total * (1.0 / S)
        for h in range(2):
            rg[:, 2 * e + h, :] = total[:, h * JP:h * JP + J]

    wait_recv(g2recv.at[pl.ds(0, NS - 1)], 8)
    for h in range(2):
        lg[:, h, :] = jnp.concatenate(
            [g2recv[q].astype(F32)[:, h * JP:h * JP + I] for q in range(NS)], axis=1
        )

    wait_recv(wall.at[pl.ds(0, NP - 1)], 7)
    for ah in range(2):
        for e in range(NE):
            x = wall[2 * e + ah].astype(F32)
            for h in range(2):
                wg[pl.ds(ah * CH * 2 * NE + 2 * e + h, CH, stride=2 * NE), :] = x[:, h * CP:(h + 1) * CP]

    wait_send(gtf.at[pl.ds(0, (NZ * NS - 1) * SB // 2)], 0)
    wait_send(rbuf.at[pl.ds(0, (NE * (NA - 1)) // NA)], 1)
    wait_send(lbuf.at[pl.ds(0, NZ)], 2)
    wait_send(grecv.at[pl.ds(0, NC - 1)], 3)
    wait_send(wrecv.at[pl.ds(0, NP - 1)], 4)
    wait_send(hrecv.at[pl.ds(0, NA - 1)], 5)
    wait_send(zrecv.at[pl.ds(0, NZ - 1)], 6)
    wait_send(wall.at[pl.ds(0, NP - 1)], 7)
    wait_send(g2recv.at[pl.ds(0, NS - 1)], 8)


def finish(*refs):
    sem = refs[8]
    copies = [pltpu.make_async_copy(refs[q], refs[4 + q], sem.at[q]) for q in range(4)]
    for copy in copies:
        copy.start()
    for copy in copies:
        copy.wait()


def body(n, left, right, projection, bias, cotangent):
    NR, NC, NS, NZ = n
    NYH = NC // NZ
    NA = NR * NS
    NP = NR * NYH * NS
    SB = left.shape[0]
    S = SB * NS
    C = 2 * NC
    CH = C // 2
    I, J, CP = cotangent.shape
    JP = 64 if J == 48 else 2 * J
    L2 = 2 * JP
    NER = right.shape[1] // 2
    NE = NER * NR

    vmem = pl.BlockSpec(memory_space=pltpu.VMEM)
    hbm = pl.BlockSpec(memory_space=pl.ANY)
    scratch = [
        pltpu.VMEM(left.shape, BF16),
        pltpu.VMEM(right.shape, BF16),
        pltpu.VMEM((SB * 2 * NER, 128), F32),
        pltpu.VMEM(cotangent.shape, BF16),
        pltpu.VMEM(projection.shape, BF16),
        pltpu.VMEM(projection.shape, F32),
        pltpu.VMEM((NE * C, 2 * CP), BF16),
        pltpu.VMEM((2 * CP, NE * C), BF16),
        pltpu.VMEM((NS, SB, L2), BF16),
        pltpu.VMEM((NER, SB, L2), BF16),
        pltpu.VMEM((NC, S, L2), BF16),
        pltpu.VMEM((2, I * CH, S), F32),
        pltpu.VMEM((S, I * C), BF16),
        pltpu.VMEM((NE, S, L2), BF16),
        pltpu.VMEM((NE * L2, S), BF16),
        pltpu.VMEM((I, 2, NE, CH, L2), BF16),
        pltpu.VMEM((I, 2, NE, CH, L2), BF16),
        pltpu.VMEM((I, L2, 2 * CP), BF16),
        pltpu.VMEM((I * C, S), F32),
        pltpu.VMEM((NC, 2 * I, S), BF16),
        pltpu.VMEM((NC, 2 * I, S), BF16),
        pltpu.VMEM((NE, S, L2), BF16),
        pltpu.VMEM((NA, NER, SB, L2), BF16),
        pltpu.VMEM((S, L2), BF16),
        pltpu.VMEM((NS, SB, L2), BF16),
        pltpu.VMEM((NP, CH, 2 * CP), BF16),
        pltpu.VMEM((NP, CH, 2 * CP), BF16),
        pltpu.VMEM((CH, 2 * CP), BF16),
        pltpu.VMEM((NZ, CH, 2 * CP), BF16),
        pltpu.VMEM((CH, 2 * CP), BF16),
        pltpu.VMEM((NP, CH, 2 * CP), BF16),
        pltpu.VMEM((NE * CH, 2 * CP), F32),
        pltpu.SemaphoreType.DMA((9,)),
        pltpu.SemaphoreType.DMA((9,)),
        pltpu.SemaphoreType.DMA((4,)),
    ]
    shapes = ((I, J, CP), BF16), (left.shape, F32), (right.shape, F32), (projection.shape, F32)
    results = pl.pallas_call(
        functools.partial(kernel, n),
        out_shape=tuple(pltpu.VMEM(shape, dtype) for shape, dtype in shapes),
        in_specs=[hbm] * 4 + [vmem],
        out_specs=(vmem,) * 4,
        scratch_shapes=scratch,
        compiler_params=pltpu.CompilerParams(
            collective_id=0, has_side_effects=True, vmem_limit_bytes=62 * 1024 * 1024
        ),
    )(left, right, cotangent, projection, bias.reshape(1, CP))
    return pl.pallas_call(
        finish,
        out_shape=tuple(jax.ShapeDtypeStruct(shape, dtype) for shape, dtype in shapes),
        in_specs=[vmem] * 4,
        out_specs=(hbm,) * 4,
        scratch_shapes=[pltpu.SemaphoreType.DMA((4,))],
        compiler_params=pltpu.CompilerParams(vmem_limit_bytes=4 * 1024 * 1024),
    )(*results)


def solution(mesh, nz=NZ):
    n = (mesh.shape["row"], mesh.shape["col"], mesh.shape["seq"], nz)
    return jax.shard_map(
        functools.partial(body, n),
        mesh=mesh,
        in_specs=(
            P("seq", "col", "row"),
            P("seq", "row", "col"),
            P(),
            P(),
            P(("row", "seq"), "col", None),
        ),
        out_specs=(
            P(("row", "seq"), "col", None),
            P("seq", "col", "row"),
            P("seq", "row", "col"),
            P(),
        ),
        check_vma=False,
    )
```

```python
import functools
import math

import jax
import jax.numpy as jnp
from jax import lax
from jax.experimental import pallas as pl
from jax.experimental.pallas import tpu as pltpu
from jax.sharding import PartitionSpec as P

MESH = pl.DeviceIdType.MESH
F32 = jnp.float32
BF16 = jnp.bfloat16
NZ = 8


def dot(a, b, dims):
    return lax.dot_general(a, b, (dims, ((), ())), preferred_element_type=F32)


def log2(size):
    return size.bit_length() - 1


NN = ((1,), (0,))
NT = ((1,), (1,))


def kernel(n, left, right, cot_in, w_in, bias_in, pair, lg, rg, wg,
           bias, leftv, rightv, rightf, cot, wv, wf, w3, w2t, xl, xr,
           lbuf, ltf, ltt, rbuf, rt, dbuf, obuf, cbd, gtf, gsend, gx, g1send, grecv, hsend, hx, h1send, hrecv,
           wsend, wrecv, w1send, zrecv, w2send, wall, wacc, ssem, rsem, nsem, fsem, lsem):
    NR, NC, NS, NZ = n
    NYH = NC // NZ
    NA = NR * NS
    NP = NR * NYH * NS
    SB = xl.shape[1]
    I, J, CP = cot.shape
    JP = xl.shape[2] // 2
    L2 = 2 * JP
    NER = xr.shape[0]
    NE = NER * NR
    C = 2 * NC
    CH = C // 2
    S = SB * NS
    IB = I

    r = lax.axis_index("row")
    c = lax.axis_index("col")
    s = lax.axis_index("seq")
    z = c & (NZ - 1)
    yh = c // NZ
    ia = r * NS + s
    ip = (r * NYH + yh) * NS + s

    def seq_peer(k):
        return (r, c, (s + k) & (NS - 1))

    def plane_device(t):
        return (t >> log2(NYH * NS), ((t >> log2(NS)) & (NYH - 1)) * NZ + z, t & (NS - 1))

    def plane_peer(k):
        return plane_device((ip + k) & (NP - 1))

    def z_peer(k):
        return (r, yh * NZ + ((z + k) & (NZ - 1)), s)

    def loop(lo, hi, f, unroll=1):
        unroll = math.gcd(hi - lo, unroll)

        def step(k, carry):
            for q in range(unroll):
                f(lo + k * unroll + q)
            return carry
        lax.fori_loop(0, (hi - lo) // unroll, step, 0)

    def send(src, dst, phase, dev):
        pltpu.make_async_remote_copy(
            src_ref=src, dst_ref=dst, send_sem=ssem.at[phase], recv_sem=rsem.at[phase],
            device_id=dev, device_id_type=MESH,
        ).start()

    def wait_recv(ref, phase):
        pltpu.make_async_copy(ref, ref, rsem.at[phase]).wait()

    def wait_send(ref, phase):
        pltpu.make_async_copy(ref, ref, ssem.at[phase]).wait()

    loads = [
        pltpu.make_async_copy(src, dst, lsem.at[q])
        for q, (src, dst) in enumerate([(left, leftv), (right, rightv), (w_in, wv), (cot_in, cot), (bias_in, bias)])
    ]
    for load in loads:
        load.start()

    barrier = pltpu.get_barrier_semaphore()

    def greet(dev):
        pl.semaphore_signal(barrier, inc=1, device_id=dev, device_id_type=MESH)

    near = sorted(range(NZ), key=lambda k: min(k, NZ - k))
    relayed = [k for k in near if min(k, NZ - k) > NZ // 4]
    direct = [k for k in near if k not in relayed]

    def greet_z(k):
        t = (z + k) & (NZ - 1)
        for q in range(NS):
            greet((r, yh * NZ + t, q))
        if k in direct:
            for q in range(NS):
                greet((r, (1 - yh) * NZ + t, q))

    def greet_row(k):
        for h in range(NYH):
            for t in range(NS):
                greet(((r + k) & (NR - 1), h * NZ + z, t))

    loop(1, NR, greet_row)
    for k in relayed[::-1] + direct[:0:-1]:
        greet_z(k)
    for k in range(1, NS):
        greet(seq_peer(k))
    for q in range(NS):
        greet((r, (1 - yh) * NZ + z, q))

    loads[0].wait()
    loads[1].wait()
    lf = leftv[...].astype(F32)
    zero = jnp.zeros((SB, JP - I), F32)
    for q in range(NS):
        parts = []
        for h in range(2):
            parts += [lf[:, h, q * I:(q + 1) * I], zero]
        xl[q] = jnp.concatenate(parts, axis=1).astype(BF16)
    rightf[:, pl.ds(0, J)] = rightv[...].astype(F32).reshape(SB * 2 * NER, J)
    for e in range(NER):
        parts = []
        for h in range(2):
            parts += [rightf[pl.ds(2 * e + h, SB, stride=2 * NER), :][:, :J], zero]
        xr[e] = jnp.concatenate(parts, axis=1).astype(BF16)

    srow = pl.multiple_of(s * SB, SB)
    erow = pl.multiple_of(r * NER, NER)

    pl.semaphore_wait(barrier, (NR - 1) * NYH * NS + (NZ - 1) * 2 * NS - len(relayed) * NS + 2 * NS - 1)

    def copy(src, dst, send_sem, recv_sem, dev):
        pltpu.make_async_remote_copy(
            src_ref=src, dst_ref=dst, send_sem=send_sem, recv_sem=recv_sem, device_id=dev, device_id_type=MESH
        ).start()

    core = s & 1
    sibling = (r, c, s + 1 - 2 * core)

    def right_to(dev):
        send(xr, rbuf.at[pl.ds(erow, NER), pl.ds(srow, SB)], 1, dev)

    for k in range(1, NR):
        for t in range(NS // 2):
            right_to(((r + k) & (NR - 1), c, 2 * t + core))
    for k in range(1, NS // 2):
        right_to((r, c, (s + 2 * k) & (NS - 1)))

    def left_to(half, k, send_sem, recv_sem):
        for t in range(NS):
            copy(xl.at[t], lbuf.at[c, pl.ds(srow, SB)], send_sem, recv_sem,
                 (r, half * NZ + ((z + k) & (NZ - 1)), t))

    arrival = relayed[::-1] + direct
    for k in arrival:
        if k == 0:
            for t in range(1, NS):
                copy(xl.at[(s + t) & (NS - 1)], lbuf.at[c, pl.ds(srow, SB)], ssem.at[0], nsem.at[0], seq_peer(t))
        else:
            left_to(yh, k, ssem.at[0], nsem.at[k])
    for k in direct:
        left_to(1 - yh, k, ssem.at[2], fsem.at[k])
    lbuf[c, pl.ds(srow, SB), :] = xl[s]
    rbuf[pl.ds(erow, NER), pl.ds(srow, SB), :] = xr[...]

    loads[2].wait()
    loads[3].wait()
    loads[4].wait()
    wf[...] = wv[...].astype(F32)
    for ah in range(2):
        for e in range(NE):
            for h in range(2):
                w3[pl.ds((ah * NE + e) * CH, CH), pl.ds(h * CP, CP)] = (
                    wf[pl.ds(ah * CH * 2 * NE + 2 * e + h, CH, stride=2 * NE), :].astype(BF16)
                )
    w2t[...] = w3[...].astype(F32).T.astype(BF16)

    def d_step(k):
        zc = jnp.zeros((JP, CP), BF16)
        for q in range(2):
            i = 2 * k + q
            a = jnp.concatenate([cot[i], jnp.zeros((JP - J, CP), BF16)], axis=0)
            cbd[i, pl.ds(0, JP), :] = jnp.concatenate([a, zc], axis=1)
            cbd[i, pl.ds(JP, JP), :] = jnp.concatenate([zc, a], axis=1)
        rhs = cbd[pl.ds(2 * k, 2)].reshape(2 * L2, 2 * CP)
        d = dot(w3[...], rhs, NT).astype(BF16)
        dbuf[2 * k] = d[:, :L2].reshape(2, NE, CH, L2)
        dbuf[2 * k + 1] = d[:, L2:].reshape(2, NE, CH, L2)

    loop(0, I // 2, d_step, 4)

    def rows_of(ah, q):
        x = lbuf[ah * NZ + q].astype(F32).T
        for h in range(2):
            ltf[ah, pl.ds(2 * q + h, I, stride=CH), :] = x[h * JP:h * JP + I]

    for k in arrival:
        q = (z + NZ - k) & (NZ - 1)
        block = lbuf.at[yh * NZ + q]
        got = lbuf.at[0, pl.ds(0, S - SB if k == 0 else S)]
        pltpu.make_async_copy(got, got, nsem.at[k]).wait()
        if k in relayed:
            copy(block, block, ssem.at[2], fsem.at[k], (r, (1 - yh) * NZ + z, s))
        rows_of(yh, q)
        if k == relayed[0]:
            wait_recv(rbuf.at[pl.ds(0, (NE * (NA // 2 - 1)) // NA)], 1)
            for t in range(NS // 2):
                part = rbuf.at[:, pl.ds(pl.multiple_of((2 * t + core) * SB, SB), SB)]
                send(part, part, 9, sibling)

    wait_recv(rbuf.at[pl.ds(0, NE // 2)], 9)

    def half_step(ah):
        lh = ltf.at[ah]

        def o_step(k):
            base = k * IB
            a = lh[pl.ds(pl.multiple_of(base * CH, IB * CH), IB * CH), :].astype(BF16)
            rhs = jnp.concatenate([rbuf[e] for e in range(NE)], axis=1)
            o = dot(a, rhs, NN).astype(BF16)
            for e in range(NE):
                obuf[pl.ds(base, IB), ah, e] = o[:, e * L2:(e + 1) * L2].reshape(IB, CH, L2)

        loop(0, I // IB, o_step)
        wacc[...] = jnp.zeros_like(wacc)

        def w_step(k):
            base = k * 8
            lhs = jnp.concatenate([obuf[base + q, ah].reshape(NE * CH, L2) for q in range(8)], axis=1)
            wacc[...] += dot(lhs, cbd[pl.ds(base, 8)].reshape(8 * L2, 2 * CP), NN)

        loop(0, I // 8, w_step, 3)
        for e in range(NE):
            wsend[2 * e + ah] = wacc[pl.ds(e * CH, CH), :].astype(BF16)

        def send_piece(k):
            t = 2 * (((ip >> 1) + k) & (NE - 1)) + ah

            @pl.when(t != ip)
            def _():
                send(wsend.at[t], wrecv.at[ip], 4, plane_device(t))

        loop(0, NE, send_piece)

    half_step(yh)

    for k in direct + relayed[::-1]:
        pltpu.make_async_copy(lbuf.at[0], lbuf.at[0], fsem.at[k]).wait()
        rows_of(1 - yh, (z + NZ - k) & (NZ - 1))
    half_step(1 - yh)
    wrecv[ip] = wsend[ip]

    for e in range(NE):
        rt[pl.ds(e * L2, L2), :] = rbuf[e].astype(F32).T.astype(BF16)

    def g_step(k):
        base = k * 8
        lhs = jnp.concatenate(
            [dbuf[pl.ds(base, 8), :, e].reshape(8 * C, L2) for e in range(NE)], axis=1
        )
        gtf[pl.ds(pl.multiple_of(base * C, 8 * C), 8 * C), :] = dot(lhs, rt[...], NN)

    loop(0, I // 8, g_step, 3)
    for q in range(NC):
        for h in range(2):
            gsend[q, pl.ds(h * I, I), :] = gtf[pl.ds(2 * q + h, I, stride=C), :].astype(BF16)

    partner = (r, (1 - yh) * NZ + z, s)
    send(gsend.at[pl.ds(pl.multiple_of((1 - yh) * NZ, NZ), NZ)], gx, 10, partner)

    for ah in range(2):
        for q in range((I * CH) // S):
            ltt[:, pl.ds((ah * I * CH) + q * S, S)] = ltf[ah, pl.ds(q * S, S), :].T.astype(BF16)

    def h_step(k):
        rhs = jnp.concatenate(
            [
                jnp.concatenate([dbuf[:, ah, 2 * k + q].reshape(I * CH, L2) for ah in range(2)], axis=0)
                for q in range(2)
            ],
            axis=1,
        )
        h = dot(ltt[...], rhs, NN).astype(BF16)
        hsend[2 * k] = h[:, :L2]
        hsend[2 * k + 1] = h[:, L2:]

    loop(0, NE // 2, h_step, 2)

    for t in range(NS // 2):
        send(hsend.at[:, pl.ds(pl.multiple_of((2 * t + 1 - core) * SB, SB), SB)], hx.at[t], 11, sibling)

    wait_recv(wrecv.at[pl.ds(0, NP - 1)], 4)
    total = wrecv[0].astype(F32)
    for q in range(1, NP):
        total = total + wrecv[q].astype(F32)
    w1send[...] = total.astype(BF16)
    loop(1, NZ, lambda k: send(w1send, zrecv.at[z], 6, z_peer(k)))
    zrecv[z] = w1send[...]

    wait_recv(hx, 11)
    for t in range(NS // 2):
        h1send[t] = (
            hsend[:, pl.ds(pl.multiple_of((2 * t + core) * SB, SB), SB), :].astype(F32) + hx[t].astype(F32)
        ).astype(BF16)
    own = r * (NS // 2) + (s >> 1)
    for k in range(1, NR):
        for t in range(NS // 2):
            q = (r + k) & (NR - 1)
            send(h1send.at[t, pl.ds(pl.multiple_of(q * NER, NER), NER)], hrecv.at[own], 5, (q, c, 2 * t + core))
    for k in range(1, NS // 2):
        t = ((s >> 1) + k) & (NS // 2 - 1)
        send(h1send.at[t, pl.ds(erow, NER)], hrecv.at[own], 5, (r, c, 2 * t + core))
    hrecv[own] = h1send[s >> 1, pl.ds(erow, NER)]

    def p_step(k):
        rhs = jnp.concatenate(
            [obuf[2 * k].reshape(NE * C, L2), obuf[2 * k + 1].reshape(NE * C, L2)], axis=1
        )
        y = dot(w2t[...], rhs, NN)
        lo, hi = y[:CP], y[CP:]
        a = lo[:, :L2] + pltpu.roll(hi[:, :L2], JP, 1)
        b = hi[:, L2:] + pltpu.roll(lo[:, L2:], JP, 1)
        lane = lax.broadcasted_iota(jnp.int32, a.shape, 1)
        m = jnp.where(lane < JP, a, b).T * (1.0 / S) + bias[...]
        m = m.astype(BF16)
        pair[2 * k] = m[:J]
        pair[2 * k + 1] = m[JP:JP + J]

    loop(0, I // 4, p_step, 4)

    wait_recv(zrecv.at[pl.ds(0, NZ - 1)], 6)
    total = zrecv[0].astype(F32)
    for q in range(1, NZ):
        total = total + zrecv[q].astype(F32)
    w2send[...] = (total * (1.0 / S)).astype(BF16)
    loop(1, NP, lambda k: send(w2send, wall.at[ip], 7, plane_peer(k)))
    wall[ip] = w2send[...]

    wait_recv(gx, 10)
    pad = jnp.zeros((JP - I, S), F32)
    for q in range(NZ):
        t = (gsend[yh * NZ + q].astype(F32) + gx[q].astype(F32)) * (1.0 / S)
        g1send[q] = jnp.concatenate([t[:I], pad, t[I:], pad], axis=0).T.astype(BF16)
    for k in range(1, NS):
        t = (s + k) & (NS - 1)
        send(g1send.at[z, pl.ds(pl.multiple_of(t * SB, SB), SB)], grecv.at[z * NS + s], 3, (r, c, t))

    def g_send(k):
        q = (z + k) & (NZ - 1)
        for t in range(NS):
            send(g1send.at[q, pl.ds(t * SB, SB)], grecv.at[z * NS + s], 3, (r, yh * NZ + q, t))

    loop(1, NZ, g_send)
    grecv[z * NS + s] = g1send[z, pl.ds(srow, SB), :]

    loop(I // 4, I // 2, p_step, 4)

    wait_recv(hrecv.at[pl.ds(0, NA // 2 - 1)], 5)
    for e in range(NER):
        total = hrecv[0, e].astype(F32)
        for q in range(1, NA // 2):
            total = total + hrecv[q, e].astype(F32)
        total = total * (1.0 / S)
        for h in range(2):
            rg[:, 2 * e + h, :] = total[:, h * JP:h * JP + J]

    wait_recv(grecv.at[pl.ds(0, NZ * NS - 1)], 3)
    parts = []
    for q in range(NS):
        total = grecv[q].astype(F32)
        for t in range(1, NZ):
            total = total + grecv[t * NS + q].astype(F32)
        parts.append(total)
    for h in range(2):
        lg[:, h, :] = jnp.concatenate([x[:, h * JP:h * JP + I] for x in parts], axis=1)

    wait_recv(wall.at[pl.ds(0, NP - 1)], 7)
    for ah in range(2):
        for e in range(NE):
            x = wall[2 * e + ah].astype(F32)
            for h in range(2):
                wg[pl.ds(ah * CH * 2 * NE + 2 * e + h, CH, stride=2 * NE), :] = x[:, h * CP:(h + 1) * CP]

    wait_send(gtf.at[pl.ds(0, (NZ * NS - 1) * SB // 2)], 0)
    wait_send(rbuf.at[pl.ds(0, (NE * (NA // 2 - 1)) // NA)], 1)
    wait_send(rbuf.at[pl.ds(0, NE // 2)], 9)
    wait_send(lbuf.at[pl.ds(0, NZ)], 2)
    wait_send(grecv.at[pl.ds(0, NZ * NS - 1)], 3)
    wait_send(gx, 10)
    wait_send(hx, 11)
    wait_send(wrecv.at[pl.ds(0, NP - 1)], 4)
    wait_send(hrecv.at[pl.ds(0, NA // 2 - 1)], 5)
    wait_send(zrecv.at[pl.ds(0, NZ - 1)], 6)
    wait_send(wall.at[pl.ds(0, NP - 1)], 7)


def finish(*refs):
    sem = refs[8]
    copies = [pltpu.make_async_copy(refs[q], refs[4 + q], sem.at[q]) for q in range(4)]
    for copy in copies:
        copy.start()
    for copy in copies:
        copy.wait()


def body(n, left, right, projection, bias, cotangent):
    NR, NC, NS, NZ = n
    NYH = NC // NZ
    NA = NR * NS
    NP = NR * NYH * NS
    SB = left.shape[0]
    S = SB * NS
    C = 2 * NC
    CH = C // 2
    I, J, CP = cotangent.shape
    JP = 64 if J == 48 else 2 * J
    L2 = 2 * JP
    NER = right.shape[1] // 2
    NE = NER * NR

    vmem = pl.BlockSpec(memory_space=pltpu.VMEM)
    hbm = pl.BlockSpec(memory_space=pl.ANY)
    scratch = [
        pltpu.VMEM((1, CP), F32),
        pltpu.VMEM(left.shape, BF16),
        pltpu.VMEM(right.shape, BF16),
        pltpu.VMEM((SB * 2 * NER, 128), F32),
        pltpu.VMEM(cotangent.shape, BF16),
        pltpu.VMEM(projection.shape, BF16),
        pltpu.VMEM(projection.shape, F32),
        pltpu.VMEM((NE * C, 2 * CP), BF16),
        pltpu.VMEM((2 * CP, NE * C), BF16),
        pltpu.VMEM((NS, SB, L2), BF16),
        pltpu.VMEM((NER, SB, L2), BF16),
        pltpu.VMEM((NC, S, L2), BF16),
        pltpu.VMEM((2, I * CH, S), F32),
        pltpu.VMEM((S, I * C), BF16),
        pltpu.VMEM((NE, S, L2), BF16),
        pltpu.VMEM((NE * L2, S), BF16),
        pltpu.VMEM((I, 2, NE, CH, L2), BF16),
        pltpu.VMEM((I, 2, NE, CH, L2), BF16),
        pltpu.VMEM((I, L2, 2 * CP), BF16),
        pltpu.VMEM((I * C, S), F32),
        pltpu.VMEM((NC, 2 * I, S), BF16),
        pltpu.VMEM((NZ, 2 * I, S), BF16),
        pltpu.VMEM((NZ, S, L2), BF16),
        pltpu.VMEM((NZ * NS, SB, L2), BF16),
        pltpu.VMEM((NE, S, L2), BF16),
        pltpu.VMEM((NS // 2, NE, SB, L2), BF16),
        pltpu.VMEM((NS // 2, NE, SB, L2), BF16),
        pltpu.VMEM((NA // 2, NER, SB, L2), BF16),
        pltpu.VMEM((NP, CH, 2 * CP), BF16),
        pltpu.VMEM((NP, CH, 2 * CP), BF16),
        pltpu.VMEM((CH, 2 * CP), BF16),
        pltpu.VMEM((NZ, CH, 2 * CP), BF16),
        pltpu.VMEM((CH, 2 * CP), BF16),
        pltpu.VMEM((NP, CH, 2 * CP), BF16),
        pltpu.VMEM((NE * CH, 2 * CP), F32),
        pltpu.SemaphoreType.DMA((12,)),
        pltpu.SemaphoreType.DMA((12,)),
        pltpu.SemaphoreType.DMA((NZ,)),
        pltpu.SemaphoreType.DMA((NZ,)),
        pltpu.SemaphoreType.DMA((5,)),
    ]
    shapes = ((I, J, CP), BF16), (left.shape, F32), (right.shape, F32), (projection.shape, F32)
    results = pl.pallas_call(
        functools.partial(kernel, n),
        out_shape=tuple(pltpu.VMEM(shape, dtype) for shape, dtype in shapes),
        in_specs=[hbm] * 5,
        out_specs=(vmem,) * 4,
        scratch_shapes=scratch,
        compiler_params=pltpu.CompilerParams(
            collective_id=0, has_side_effects=True, vmem_limit_bytes=62 * 1024 * 1024
        ),
    )(left, right, cotangent, projection, bias.reshape(1, CP))
    return pl.pallas_call(
        finish,
        out_shape=tuple(jax.ShapeDtypeStruct(shape, dtype) for shape, dtype in shapes),
        in_specs=[vmem] * 4,
        out_specs=(hbm,) * 4,
        scratch_shapes=[pltpu.SemaphoreType.DMA((4,))],
        compiler_params=pltpu.CompilerParams(vmem_limit_bytes=4 * 1024 * 1024),
    )(*results)


def solution(mesh, nz=NZ):
    n = (mesh.shape["row"], mesh.shape["col"], mesh.shape["seq"], nz)
    return jax.shard_map(
        functools.partial(body, n),
        mesh=mesh,
        in_specs=(
            P("seq", "col", "row"),
            P("seq", "row", "col"),
            P(),
            P(),
            P(("row", "seq"), "col", None),
        ),
        out_specs=(
            P(("row", "seq"), "col", None),
            P("seq", "col", "row"),
            P("seq", "row", "col"),
            P(),
        ),
        check_vma=False,
    )
```

```python
import functools
import math

import jax
import jax.numpy as jnp
from jax import lax
from jax.experimental import pallas as pl
from jax.experimental.pallas import tpu as pltpu
from jax.sharding import PartitionSpec as P

MESH = pl.DeviceIdType.MESH
F32 = jnp.float32
BF16 = jnp.bfloat16
NZ = 8


def dot(a, b, dims):
    return lax.dot_general(a, b, (dims, ((), ())), preferred_element_type=F32)


def log2(size):
    return size.bit_length() - 1


NN = ((1,), (0,))
NT = ((1,), (1,))


def kernel(n, left, right, cot_in, w_in, bias_in, pair, lg, rg, wg,
           bias, leftv, rightv, rightf, cot, wv, wf, w3, w2t, xl, xr,
           lbuf, ltf, ltt, rbuf, rt, dbuf, obuf, cbd, gtf, gsend, gx, g1send, grecv, hsend, hx, h1send, hrecv,
           wsend, wrecv, w1send, zrecv, w2send, wall, wacc, ssem, rsem, nsem, fsem, lsem):
    NR, NC, NS, NZ = n
    NYH = NC // NZ
    NA = NR * NS
    NP = NR * NYH * NS
    SB = xl.shape[1]
    I, J, CP = cot.shape
    JP = xl.shape[2] // 2
    L2 = 2 * JP
    NER = xr.shape[0]
    NE = NER * NR
    C = 2 * NC
    CH = C // 2
    S = SB * NS
    IB = I

    r = lax.axis_index("row")
    c = lax.axis_index("col")
    s = lax.axis_index("seq")
    z = c & (NZ - 1)
    yh = c // NZ
    ia = r * NS + s
    ip = (r * NYH + yh) * NS + s

    def seq_peer(k):
        return (r, c, (s + k) & (NS - 1))

    def plane_device(t):
        return (t >> log2(NYH * NS), ((t >> log2(NS)) & (NYH - 1)) * NZ + z, t & (NS - 1))

    def plane_peer(k):
        return plane_device((ip + k) & (NP - 1))

    def z_peer(k):
        return (r, yh * NZ + ((z + k) & (NZ - 1)), s)

    def loop(lo, hi, f, unroll=1):
        unroll = math.gcd(hi - lo, unroll)

        def step(k, carry):
            for q in range(unroll):
                f(lo + k * unroll + q)
            return carry
        lax.fori_loop(0, (hi - lo) // unroll, step, 0)

    def send(src, dst, phase, dev):
        pltpu.make_async_remote_copy(
            src_ref=src, dst_ref=dst, send_sem=ssem.at[phase], recv_sem=rsem.at[phase],
            device_id=dev, device_id_type=MESH,
        ).start()

    def wait_recv(ref, phase):
        pltpu.make_async_copy(ref, ref, rsem.at[phase]).wait()

    def wait_send(ref, phase):
        pltpu.make_async_copy(ref, ref, ssem.at[phase]).wait()

    loads = [
        pltpu.make_async_copy(src, dst, lsem.at[q])
        for q, (src, dst) in enumerate([(left, leftv), (right, rightv), (w_in, wv), (cot_in, cot), (bias_in, bias)])
    ]
    for load in loads:
        load.start()

    barrier = pltpu.get_barrier_semaphore()

    def greet(dev):
        pl.semaphore_signal(barrier, inc=1, device_id=dev, device_id_type=MESH)

    near = sorted(range(NZ), key=lambda k: min(k, NZ - k))
    relayed = [k for k in near if min(k, NZ - k) > NZ // 4]
    direct = [k for k in near if k not in relayed]
    NG = NZ + len(direct)

    def greet_z(k):
        t = (z + k) & (NZ - 1)
        for q in range(NS):
            greet((r, yh * NZ + t, q))
        if k in direct:
            for q in range(NS):
                greet((r, (1 - yh) * NZ + t, q))

    def greet_row(k):
        for h in range(NYH):
            for t in range(NS):
                greet(((r + k) & (NR - 1), h * NZ + z, t))

    loop(1, NR, greet_row)
    for k in relayed[::-1] + direct[:0:-1]:
        greet_z(k)
    for k in range(1, NS):
        greet(seq_peer(k))
    for q in range(NS):
        greet((r, (1 - yh) * NZ + z, q))

    loads[0].wait()
    loads[1].wait()
    lf = leftv[...].astype(F32)
    zero = jnp.zeros((SB, JP - I), F32)
    for q in range(NS):
        parts = []
        for h in range(2):
            parts += [lf[:, h, q * I:(q + 1) * I], zero]
        xl[q] = jnp.concatenate(parts, axis=1).astype(BF16)
    rightf[:, pl.ds(0, J)] = rightv[...].astype(F32).reshape(SB * 2 * NER, J)
    for e in range(NER):
        parts = []
        for h in range(2):
            parts += [rightf[pl.ds(2 * e + h, SB, stride=2 * NER), :][:, :J], zero]
        xr[e] = jnp.concatenate(parts, axis=1).astype(BF16)

    srow = pl.multiple_of(s * SB, SB)
    erow = pl.multiple_of(r * NER, NER)

    pl.semaphore_wait(barrier, (NR - 1) * NYH * NS + (NZ - 1) * 2 * NS - len(relayed) * NS + 2 * NS - 1)

    def copy(src, dst, send_sem, recv_sem, dev):
        pltpu.make_async_remote_copy(
            src_ref=src, dst_ref=dst, send_sem=send_sem, recv_sem=recv_sem, device_id=dev, device_id_type=MESH
        ).start()

    core = s & 1
    sibling = (r, c, s + 1 - 2 * core)

    def right_to(dev):
        send(xr, rbuf.at[pl.ds(erow, NER), pl.ds(srow, SB)], 1, dev)

    for k in range(1, NR):
        for t in range(NS // 2):
            right_to(((r + k) & (NR - 1), c, 2 * t + core))
    for k in range(1, NS // 2):
        right_to((r, c, (s + 2 * k) & (NS - 1)))

    def left_to(half, k, send_sem, recv_sem):
        for t in range(NS):
            copy(xl.at[t], lbuf.at[c, pl.ds(srow, SB)], send_sem, recv_sem,
                 (r, half * NZ + ((z + k) & (NZ - 1)), t))

    arrival = relayed[::-1] + direct
    for k in arrival:
        if k == 0:
            for t in range(1, NS):
                copy(xl.at[(s + t) & (NS - 1)], lbuf.at[c, pl.ds(srow, SB)], ssem.at[0], nsem.at[0], seq_peer(t))
        else:
            left_to(yh, k, ssem.at[0], nsem.at[k])
    for k in direct:
        left_to(1 - yh, k, ssem.at[2], fsem.at[k])
    lbuf[c, pl.ds(srow, SB), :] = xl[s]
    rbuf[pl.ds(erow, NER), pl.ds(srow, SB), :] = xr[...]

    loads[2].wait()
    loads[3].wait()
    loads[4].wait()
    wf[...] = wv[...].astype(F32)
    for ah in range(2):
        for e in range(NE):
            for h in range(2):
                w3[pl.ds((ah * NE + e) * CH, CH), pl.ds(h * CP, CP)] = (
                    wf[pl.ds(ah * CH * 2 * NE + 2 * e + h, CH, stride=2 * NE), :].astype(BF16)
                )
    w2t[...] = w3[...].astype(F32).T.astype(BF16)

    def d_step(k):
        zc = jnp.zeros((JP, CP), BF16)
        for q in range(2):
            i = 2 * k + q
            a = jnp.concatenate([cot[i], jnp.zeros((JP - J, CP), BF16)], axis=0)
            cbd[i, pl.ds(0, JP), :] = jnp.concatenate([a, zc], axis=1)
            cbd[i, pl.ds(JP, JP), :] = jnp.concatenate([zc, a], axis=1)
        rhs = cbd[pl.ds(2 * k, 2)].reshape(2 * L2, 2 * CP)
        d = dot(w3[...], rhs, NT).astype(BF16)
        dbuf[2 * k] = d[:, :L2].reshape(2, NE, CH, L2)
        dbuf[2 * k + 1] = d[:, L2:].reshape(2, NE, CH, L2)

    loop(0, I // 2, d_step, 4)

    def rows_of(ah, q):
        x = lbuf[ah * NZ + q].astype(F32).T
        for h in range(2):
            ltf[ah, pl.ds(2 * q + h, I, stride=CH), :] = x[h * JP:h * JP + I]

    for k in arrival:
        q = (z + NZ - k) & (NZ - 1)
        block = lbuf.at[yh * NZ + q]
        got = lbuf.at[0, pl.ds(0, S - SB if k == 0 else S)]
        pltpu.make_async_copy(got, got, nsem.at[k]).wait()
        if k in relayed:
            copy(block, block, ssem.at[2], fsem.at[k], (r, (1 - yh) * NZ + z, s))
        rows_of(yh, q)
        if k == relayed[0]:
            wait_recv(rbuf.at[pl.ds(0, (NE * (NA // 2 - 1)) // NA)], 1)
            for t in range(NS // 2):
                part = rbuf.at[:, pl.ds(pl.multiple_of((2 * t + core) * SB, SB), SB)]
                send(part, part, 9, sibling)

    wait_recv(rbuf.at[pl.ds(0, NE // 2)], 9)

    def half_step(ah):
        lh = ltf.at[ah]

        def o_step(k):
            base = k * IB
            a = lh[pl.ds(pl.multiple_of(base * CH, IB * CH), IB * CH), :].astype(BF16)
            rhs = jnp.concatenate([rbuf[e] for e in range(NE)], axis=1)
            o = dot(a, rhs, NN).astype(BF16)
            for e in range(NE):
                obuf[pl.ds(base, IB), ah, e] = o[:, e * L2:(e + 1) * L2].reshape(IB, CH, L2)

        loop(0, I // IB, o_step)
        wacc[...] = jnp.zeros_like(wacc)

        def w_step(k):
            base = k * 8
            lhs = jnp.concatenate([obuf[base + q, ah].reshape(NE * CH, L2) for q in range(8)], axis=1)
            wacc[...] += dot(lhs, cbd[pl.ds(base, 8)].reshape(8 * L2, 2 * CP), NN)

        loop(0, I // 8, w_step, 3)
        for e in range(NE):
            wsend[2 * e + ah] = wacc[pl.ds(e * CH, CH), :].astype(BF16)

        def send_piece(k):
            t = 2 * (((ip >> 1) + k) & (NE - 1)) + ah

            @pl.when(t != ip)
            def _():
                send(wsend.at[t], wrecv.at[ip], 4, plane_device(t))

        loop(0, NE, send_piece)

    half_step(yh)

    for k in direct + relayed[::-1]:
        pltpu.make_async_copy(lbuf.at[0], lbuf.at[0], fsem.at[k]).wait()
        rows_of(1 - yh, (z + NZ - k) & (NZ - 1))
    half_step(1 - yh)
    wrecv[ip] = wsend[ip]

    for e in range(NE):
        rt[pl.ds(e * L2, L2), :] = rbuf[e].astype(F32).T.astype(BF16)

    def g_step(k):
        base = k * 8
        lhs = jnp.concatenate(
            [dbuf[pl.ds(base, 8), :, e].reshape(8 * C, L2) for e in range(NE)], axis=1
        )
        gtf[pl.ds(pl.multiple_of(base * C, 8 * C), 8 * C), :] = dot(lhs, rt[...], NN)

    loop(0, I // 8, g_step, 3)

    def g_rows(half, k):
        q = half * NZ + ((z + k) & (NZ - 1))
        return [gtf[pl.ds(2 * q + h, I, stride=C), :] for h in range(2)]

    for j, k in enumerate(relayed):
        gsend[j] = jnp.concatenate(g_rows(1 - yh, k), axis=0).astype(BF16)
    send(gsend, gx, 10, (r, (1 - yh) * NZ + z, s))

    pad = jnp.zeros((JP - I, S), F32)

    def g_block(rows):
        return (jnp.concatenate([rows[0], pad, rows[1], pad], axis=0) * (1.0 / S)).T.astype(BF16)

    for j, k in enumerate(direct):
        g1send[k] = g_block(g_rows(yh, k))
        g1send[NZ + j] = g_block(g_rows(1 - yh, k))

    def g_to(half, k, slot):
        q = (z + k) & (NZ - 1)
        for t in range(NS):
            send(g1send.at[slot, pl.ds(t * SB, SB)], grecv.at[slot * NS + s], 3, (r, half * NZ + q, t))

    for k in range(1, NS):
        t = (s + k) & (NS - 1)
        send(g1send.at[0, pl.ds(pl.multiple_of(t * SB, SB), SB)], grecv.at[s], 3, (r, c, t))
    grecv[s] = g1send[0, pl.ds(srow, SB), :]
    for j, k in enumerate(direct):
        if k > 0:
            g_to(yh, k, k)
        g_to(1 - yh, k, NZ + j)

    for ah in range(2):
        for q in range((I * CH) // S):
            ltt[:, pl.ds((ah * I * CH) + q * S, S)] = ltf[ah, pl.ds(q * S, S), :].T.astype(BF16)

    def h_step(k):
        rhs = jnp.concatenate(
            [
                jnp.concatenate([dbuf[:, ah, 2 * k + q].reshape(I * CH, L2) for ah in range(2)], axis=0)
                for q in range(2)
            ],
            axis=1,
        )
        h = dot(ltt[...], rhs, NN).astype(BF16)
        hsend[2 * k] = h[:, :L2]
        hsend[2 * k + 1] = h[:, L2:]

    loop(0, NE // 2, h_step, 2)

    for t in range(NS // 2):
        send(hsend.at[:, pl.ds(pl.multiple_of((2 * t + 1 - core) * SB, SB), SB)], hx.at[t], 11, sibling)

    wait_recv(wrecv.at[pl.ds(0, NP - 1)], 4)
    total = wrecv[0].astype(F32)
    for q in range(1, NP):
        total = total + wrecv[q].astype(F32)
    w1send[...] = total.astype(BF16)
    loop(1, NZ, lambda k: send(w1send, zrecv.at[z], 6, z_peer(k)))
    zrecv[z] = w1send[...]
    wait_recv(hx, 11)
    for t in range(NS // 2):
        h1send[t] = (
            hsend[:, pl.ds(pl.multiple_of((2 * t + core) * SB, SB), SB), :].astype(F32) + hx[t].astype(F32)
        ).astype(BF16)
    own = r * (NS // 2) + (s >> 1)
    for k in range(1, NR):
        for t in range(NS // 2):
            q = (r + k) & (NR - 1)
            send(h1send.at[t, pl.ds(pl.multiple_of(q * NER, NER), NER)], hrecv.at[own], 5, (q, c, 2 * t + core))
    for k in range(1, NS // 2):
        t = ((s >> 1) + k) & (NS // 2 - 1)
        send(h1send.at[t, pl.ds(erow, NER)], hrecv.at[own], 5, (r, c, 2 * t + core))
    hrecv[own] = h1send[s >> 1, pl.ds(erow, NER)]

    def p_step(k):
        rhs = jnp.concatenate(
            [obuf[2 * k].reshape(NE * C, L2), obuf[2 * k + 1].reshape(NE * C, L2)], axis=1
        )
        y = dot(w2t[...], rhs, NN)
        lo, hi = y[:CP], y[CP:]
        a = lo[:, :L2] + pltpu.roll(hi[:, :L2], JP, 1)
        b = hi[:, L2:] + pltpu.roll(lo[:, L2:], JP, 1)
        lane = lax.broadcasted_iota(jnp.int32, a.shape, 1)
        m = jnp.where(lane < JP, a, b).T * (1.0 / S) + bias[...]
        m = m.astype(BF16)
        pair[2 * k] = m[:J]
        pair[2 * k + 1] = m[JP:JP + J]

    loop(0, I // 4, p_step, 4)

    wait_recv(gx, 10)
    for j, k in enumerate(relayed):
        rows = g_rows(yh, k)
        g1send[k] = g_block([rows[h] + gx[j, pl.ds(h * I, I), :].astype(F32) for h in range(2)])
        g_to(yh, k, k)

    wait_recv(zrecv.at[pl.ds(0, NZ - 1)], 6)
    total = zrecv[0].astype(F32)
    for q in range(1, NZ):
        total = total + zrecv[q].astype(F32)
    w2send[...] = (total * (1.0 / S)).astype(BF16)
    loop(1, NP, lambda k: send(w2send, wall.at[ip], 7, plane_peer(k)))
    wall[ip] = w2send[...]

    loop(I // 4, I // 2, p_step, 4)

    wait_recv(hrecv.at[pl.ds(0, NA // 2 - 1)], 5)
    for e in range(NER):
        total = hrecv[0, e].astype(F32)
        for q in range(1, NA // 2):
            total = total + hrecv[q, e].astype(F32)
        total = total * (1.0 / S)
        for h in range(2):
            rg[:, 2 * e + h, :] = total[:, h * JP:h * JP + J]

    wait_recv(wall.at[pl.ds(0, NP - 1)], 7)
    for ah in range(2):
        for e in range(NE):
            x = wall[2 * e + ah].astype(F32)
            for h in range(2):
                wg[pl.ds(ah * CH * 2 * NE + 2 * e + h, CH, stride=2 * NE), :] = x[:, h * CP:(h + 1) * CP]

    wait_recv(grecv.at[pl.ds(0, NG * NS - 1)], 3)
    parts = []
    for q in range(NS):
        total = grecv[q].astype(F32)
        for t in range(1, NG):
            total = total + grecv[t * NS + q].astype(F32)
        parts.append(total)
    for h in range(2):
        lg[:, h, :] = jnp.concatenate([x[:, h * JP:h * JP + I] for x in parts], axis=1)

    wait_send(gtf.at[pl.ds(0, (NZ * NS - 1) * SB // 2)], 0)
    wait_send(rbuf.at[pl.ds(0, (NE * (NA // 2 - 1)) // NA)], 1)
    wait_send(rbuf.at[pl.ds(0, NE // 2)], 9)
    wait_send(lbuf.at[pl.ds(0, NZ)], 2)
    wait_send(grecv.at[pl.ds(0, NG * NS - 1)], 3)
    wait_send(gx, 10)
    wait_send(hx, 11)
    wait_send(wrecv.at[pl.ds(0, NP - 1)], 4)
    wait_send(hrecv.at[pl.ds(0, NA // 2 - 1)], 5)
    wait_send(zrecv.at[pl.ds(0, NZ - 1)], 6)
    wait_send(wall.at[pl.ds(0, NP - 1)], 7)


def finish(*refs):
    sem = refs[8]
    copies = [pltpu.make_async_copy(refs[q], refs[4 + q], sem.at[q]) for q in range(4)]
    for copy in copies:
        copy.start()
    for copy in copies:
        copy.wait()


def body(n, left, right, projection, bias, cotangent):
    NR, NC, NS, NZ = n
    NYH = NC // NZ
    NA = NR * NS
    NP = NR * NYH * NS
    SB = left.shape[0]
    S = SB * NS
    C = 2 * NC
    CH = C // 2
    I, J, CP = cotangent.shape
    JP = 64 if J == 48 else 2 * J
    L2 = 2 * JP
    NER = right.shape[1] // 2
    NE = NER * NR

    far = sum(min(k, NZ - k) > NZ // 4 for k in range(NZ))

    vmem = pl.BlockSpec(memory_space=pltpu.VMEM)
    hbm = pl.BlockSpec(memory_space=pl.ANY)
    scratch = [
        pltpu.VMEM((1, CP), F32),
        pltpu.VMEM(left.shape, BF16),
        pltpu.VMEM(right.shape, BF16),
        pltpu.VMEM((SB * 2 * NER, 128), F32),
        pltpu.VMEM(cotangent.shape, BF16),
        pltpu.VMEM(projection.shape, BF16),
        pltpu.VMEM(projection.shape, F32),
        pltpu.VMEM((NE * C, 2 * CP), BF16),
        pltpu.VMEM((2 * CP, NE * C), BF16),
        pltpu.VMEM((NS, SB, L2), BF16),
        pltpu.VMEM((NER, SB, L2), BF16),
        pltpu.VMEM((NC, S, L2), BF16),
        pltpu.VMEM((2, I * CH, S), F32),
        pltpu.VMEM((S, I * C), BF16),
        pltpu.VMEM((NE, S, L2), BF16),
        pltpu.VMEM((NE * L2, S), BF16),
        pltpu.VMEM((I, 2, NE, CH, L2), BF16),
        pltpu.VMEM((I, 2, NE, CH, L2), BF16),
        pltpu.VMEM((I, L2, 2 * CP), BF16),
        pltpu.VMEM((I * C, S), F32),
        pltpu.VMEM((far, 2 * I, S), BF16),
        pltpu.VMEM((far, 2 * I, S), BF16),
        pltpu.VMEM((2 * NZ - far, S, L2), BF16),
        pltpu.VMEM(((2 * NZ - far) * NS, SB, L2), BF16),
        pltpu.VMEM((NE, S, L2), BF16),
        pltpu.VMEM((NS // 2, NE, SB, L2), BF16),
        pltpu.VMEM((NS // 2, NE, SB, L2), BF16),
        pltpu.VMEM((NA // 2, NER, SB, L2), BF16),
        pltpu.VMEM((NP, CH, 2 * CP), BF16),
        pltpu.VMEM((NP, CH, 2 * CP), BF16),
        pltpu.VMEM((CH, 2 * CP), BF16),
        pltpu.VMEM((NZ, CH, 2 * CP), BF16),
        pltpu.VMEM((CH, 2 * CP), BF16),
        pltpu.VMEM((NP, CH, 2 * CP), BF16),
        pltpu.VMEM((NE * CH, 2 * CP), F32),
        pltpu.SemaphoreType.DMA((12,)),
        pltpu.SemaphoreType.DMA((12,)),
        pltpu.SemaphoreType.DMA((NZ,)),
        pltpu.SemaphoreType.DMA((NZ,)),
        pltpu.SemaphoreType.DMA((5,)),
    ]
    shapes = ((I, J, CP), BF16), (left.shape, F32), (right.shape, F32), (projection.shape, F32)
    results = pl.pallas_call(
        functools.partial(kernel, n),
        out_shape=tuple(pltpu.VMEM(shape, dtype) for shape, dtype in shapes),
        in_specs=[hbm] * 5,
        out_specs=(vmem,) * 4,
        scratch_shapes=scratch,
        compiler_params=pltpu.CompilerParams(
            collective_id=0, has_side_effects=True, vmem_limit_bytes=62 * 1024 * 1024
        ),
    )(left, right, cotangent, projection, bias.reshape(1, CP))
    return pl.pallas_call(
        finish,
        out_shape=tuple(jax.ShapeDtypeStruct(shape, dtype) for shape, dtype in shapes),
        in_specs=[vmem] * 4,
        out_specs=(hbm,) * 4,
        scratch_shapes=[pltpu.SemaphoreType.DMA((4,))],
        compiler_params=pltpu.CompilerParams(vmem_limit_bytes=4 * 1024 * 1024),
    )(*results)


def solution(mesh, nz=NZ):
    n = (mesh.shape["row"], mesh.shape["col"], mesh.shape["seq"], nz)
    return jax.shard_map(
        functools.partial(body, n),
        mesh=mesh,
        in_specs=(
            P("seq", "col", "row"),
            P("seq", "row", "col"),
            P(),
            P(),
            P(("row", "seq"), "col", None),
        ),
        out_specs=(
            P(("row", "seq"), "col", None),
            P("seq", "col", "row"),
            P("seq", "row", "col"),
            P(),
        ),
        check_vma=False,
    )
```

```python
import functools
import math

import jax
import jax.numpy as jnp
from jax import lax
from jax.experimental import pallas as pl
from jax.experimental.pallas import tpu as pltpu
from jax.sharding import PartitionSpec as P

MESH = pl.DeviceIdType.MESH
F32 = jnp.float32
BF16 = jnp.bfloat16
NZ = 8


def dot(a, b, dims):
    return lax.dot_general(a, b, (dims, ((), ())), preferred_element_type=F32)


def log2(size):
    return size.bit_length() - 1


NN = ((1,), (0,))
NT = ((1,), (1,))


def kernel(n, left, right, cot_in, w_in, bias_in, pair, lg, rg, wg,
           bias, leftv, rightv, rightf, cot, wv, wf, w3, w2t, xl, xr,
           lbuf, ltf, ltt, rbuf, rt, dbuf, obuf, cbd, gtf, gsend, gx, g1send, grecv, hsend, hx, h1send, hrecv,
           wsend, wrecv, w1send, zrecv, w2send, wall, wacc, ssem, rsem, nsem, fsem, lsem):
    NR, NC, NS, NZ = n
    NYH = NC // NZ
    NA = NR * NS
    NP = NR * NYH * NS
    SB = xl.shape[1]
    I, J, CP = cot.shape
    JP = xl.shape[2] // 2
    L2 = 2 * JP
    NER = xr.shape[0]
    NE = NER * NR
    C = 2 * NC
    CH = C // 2
    S = SB * NS
    IB = I

    r = lax.axis_index("row")
    c = lax.axis_index("col")
    s = lax.axis_index("seq")
    z = c & (NZ - 1)
    yh = c // NZ
    ia = r * NS + s
    ip = (r * NYH + yh) * NS + s

    def seq_peer(k):
        return (r, c, (s + k) & (NS - 1))

    def plane_device(t):
        return (t >> log2(NYH * NS), ((t >> log2(NS)) & (NYH - 1)) * NZ + z, t & (NS - 1))

    def plane_peer(k):
        return plane_device((ip + k) & (NP - 1))

    def z_peer(k):
        return (r, yh * NZ + ((z + k) & (NZ - 1)), s)

    def loop(lo, hi, f, unroll=1):
        unroll = math.gcd(hi - lo, unroll)

        def step(k, carry):
            for q in range(unroll):
                f(lo + k * unroll + q)
            return carry
        lax.fori_loop(0, (hi - lo) // unroll, step, 0)

    def send(src, dst, phase, dev):
        pltpu.make_async_remote_copy(
            src_ref=src, dst_ref=dst, send_sem=ssem.at[phase], recv_sem=rsem.at[phase],
            device_id=dev, device_id_type=MESH,
        ).start()

    def wait_recv(ref, phase):
        pltpu.make_async_copy(ref, ref, rsem.at[phase]).wait()

    def wait_send(ref, phase):
        pltpu.make_async_copy(ref, ref, ssem.at[phase]).wait()

    loads = [
        pltpu.make_async_copy(src, dst, lsem.at[q])
        for q, (src, dst) in enumerate([(left, leftv), (right, rightv), (w_in, wv), (cot_in, cot), (bias_in, bias)])
    ]
    for load in loads:
        load.start()

    barrier = pltpu.get_barrier_semaphore()

    def greet(dev):
        pl.semaphore_signal(barrier, inc=1, device_id=dev, device_id_type=MESH)

    near = sorted(range(NZ), key=lambda k: min(k, NZ - k))
    relayed = [k for k in near if min(k, NZ - k) > NZ // 4]
    direct = [k for k in near if k not in relayed]
    NG = NZ + len(direct)

    def greet_z(k):
        t = (z + k) & (NZ - 1)
        for q in range(NS):
            greet((r, yh * NZ + t, q))
        if k in direct:
            for q in range(NS):
                greet((r, (1 - yh) * NZ + t, q))

    def greet_row(k):
        for h in range(NYH):
            for t in range(NS):
                greet(((r + k) & (NR - 1), h * NZ + z, t))

    loop(1, NR, greet_row)
    for k in relayed[::-1] + direct[:0:-1]:
        greet_z(k)
    for k in range(1, NS):
        greet(seq_peer(k))
    for q in range(NS):
        greet((r, (1 - yh) * NZ + z, q))

    loads[0].wait()
    loads[1].wait()
    lf = leftv[...].astype(F32)
    zero = jnp.zeros((SB, JP - I), F32)
    for q in range(NS):
        parts = []
        for h in range(2):
            parts += [lf[:, h, q * I:(q + 1) * I], zero]
        xl[q] = jnp.concatenate(parts, axis=1).astype(BF16)
    rightf[:, pl.ds(0, J)] = rightv[...].astype(F32).reshape(SB * 2 * NER, J)
    for e in range(NER):
        parts = []
        for h in range(2):
            parts += [rightf[pl.ds(2 * e + h, SB, stride=2 * NER), :][:, :J], zero]
        xr[e] = jnp.concatenate(parts, axis=1).astype(BF16)

    srow = pl.multiple_of(s * SB, SB)
    erow = pl.multiple_of(r * NER, NER)

    pl.semaphore_wait(barrier, (NR - 1) * NYH * NS + (NZ - 1) * 2 * NS - len(relayed) * NS + 2 * NS - 1)

    def copy(src, dst, send_sem, recv_sem, dev):
        pltpu.make_async_remote_copy(
            src_ref=src, dst_ref=dst, send_sem=send_sem, recv_sem=recv_sem, device_id=dev, device_id_type=MESH
        ).start()

    core = s & 1
    sibling = (r, c, s + 1 - 2 * core)

    def right_to(dev):
        send(xr, rbuf.at[pl.ds(erow, NER), pl.ds(srow, SB)], 1, dev)

    for k in range(1, NR):
        for t in range(NS // 2):
            right_to(((r + k) & (NR - 1), c, 2 * t + core))
    for k in range(1, NS // 2):
        right_to((r, c, (s + 2 * k) & (NS - 1)))

    def left_to(half, k, send_sem, recv_sem):
        for t in range(NS):
            copy(xl.at[t], lbuf.at[c, pl.ds(srow, SB)], send_sem, recv_sem,
                 (r, half * NZ + ((z + k) & (NZ - 1)), t))

    arrival = relayed[::-1] + direct
    for k in arrival:
        if k == 0:
            for t in range(1, NS):
                copy(xl.at[(s + t) & (NS - 1)], lbuf.at[c, pl.ds(srow, SB)], ssem.at[0], nsem.at[0], seq_peer(t))
        else:
            left_to(yh, k, ssem.at[0], nsem.at[k])
    for k in direct:
        left_to(1 - yh, k, ssem.at[2], fsem.at[k])
    lbuf[c, pl.ds(srow, SB), :] = xl[s]
    rbuf[pl.ds(erow, NER), pl.ds(srow, SB), :] = xr[...]

    loads[2].wait()
    loads[3].wait()
    loads[4].wait()
    wf[...] = wv[...].astype(F32)
    for ah in range(2):
        for e in range(NE):
            for h in range(2):
                w3[pl.ds((ah * NE + e) * CH, CH), pl.ds(h * CP, CP)] = (
                    wf[pl.ds(ah * CH * 2 * NE + 2 * e + h, CH, stride=2 * NE), :].astype(BF16)
                )
    w2t[...] = w3[...].astype(F32).T.astype(BF16)

    def d_step(k):
        zc = jnp.zeros((JP, CP), BF16)
        for q in range(2):
            i = 2 * k + q
            a = jnp.concatenate([cot[i], jnp.zeros((JP - J, CP), BF16)], axis=0)
            cbd[i, pl.ds(0, JP), :] = jnp.concatenate([a, zc], axis=1)
            cbd[i, pl.ds(JP, JP), :] = jnp.concatenate([zc, a], axis=1)
        rhs = cbd[pl.ds(2 * k, 2)].reshape(2 * L2, 2 * CP)
        d = dot(w3[...], rhs, NT).astype(BF16)
        dbuf[2 * k] = d[:, :L2].reshape(2, NE, CH, L2)
        dbuf[2 * k + 1] = d[:, L2:].reshape(2, NE, CH, L2)

    loop(0, I // 2, d_step, 4)

    def rows_of(ah, q):
        x = lbuf[ah * NZ + q].astype(F32).T
        for h in range(2):
            ltf[ah, pl.ds(2 * q + h, I, stride=CH), :] = x[h * JP:h * JP + I]

    for k in arrival:
        q = (z + NZ - k) & (NZ - 1)
        block = lbuf.at[yh * NZ + q]
        got = lbuf.at[0, pl.ds(0, S - SB if k == 0 else S)]
        pltpu.make_async_copy(got, got, nsem.at[k]).wait()
        if k in relayed:
            copy(block, block, ssem.at[2], fsem.at[k], (r, (1 - yh) * NZ + z, s))
        rows_of(yh, q)
        if k == relayed[0]:
            wait_recv(rbuf.at[pl.ds(0, (NE * (NA // 2 - 1)) // NA)], 1)
            for t in range(NS // 2):
                part = rbuf.at[:, pl.ds(pl.multiple_of((2 * t + core) * SB, SB), SB)]
                send(part, part, 9, sibling)

    wait_recv(rbuf.at[pl.ds(0, NE // 2)], 9)

    def half_step(ah):
        lh = ltf.at[ah]

        def o_step(k):
            base = k * IB
            a = lh[pl.ds(pl.multiple_of(base * CH, IB * CH), IB * CH), :].astype(BF16)
            rhs = jnp.concatenate([rbuf[e] for e in range(NE)], axis=1)
            o = dot(a, rhs, NN).astype(BF16)
            for e in range(NE):
                obuf[pl.ds(base, IB), ah, e] = o[:, e * L2:(e + 1) * L2].reshape(IB, CH, L2)

        loop(0, I // IB, o_step)
        wacc[...] = jnp.zeros_like(wacc)

        def w_step(k):
            base = k * 8
            lhs = jnp.concatenate([obuf[base + q, ah].reshape(NE * CH, L2) for q in range(8)], axis=1)
            wacc[...] += dot(lhs, cbd[pl.ds(base, 8)].reshape(8 * L2, 2 * CP), NN)

        loop(0, I // 8, w_step, 3)
        for e in range(NE):
            wsend[2 * e + ah] = wacc[pl.ds(e * CH, CH), :].astype(BF16)

        def send_piece(k):
            t = 2 * (((ip >> 1) + k) & (NE - 1)) + ah

            @pl.when(t != ip)
            def _():
                send(wsend.at[t], wrecv.at[ip], 4, plane_device(t))

        loop(0, NE, send_piece)

    half_step(yh)

    for k in direct + relayed[::-1]:
        pltpu.make_async_copy(lbuf.at[0], lbuf.at[0], fsem.at[k]).wait()
        rows_of(1 - yh, (z + NZ - k) & (NZ - 1))
    half_step(1 - yh)
    wrecv[ip] = wsend[ip]

    for e in range(NE):
        rt[pl.ds(e * L2, L2), :] = rbuf[e].astype(F32).T.astype(BF16)

    def g_step(k):
        base = k * 8
        lhs = jnp.concatenate(
            [dbuf[pl.ds(base, 8), :, e].reshape(8 * C, L2) for e in range(NE)], axis=1
        )
        gtf[pl.ds(pl.multiple_of(base * C, 8 * C), 8 * C), :] = dot(lhs, rt[...], NN)

    loop(0, I // 8, g_step, 3)

    def g_rows(half, k):
        q = half * NZ + ((z + k) & (NZ - 1))
        return [gtf[pl.ds(2 * q + h, I, stride=C), :] for h in range(2)]

    for j, k in enumerate(relayed):
        gsend[j] = jnp.concatenate(g_rows(1 - yh, k), axis=0).astype(BF16)
    send(gsend, gx, 10, (r, (1 - yh) * NZ + z, s))

    pad = jnp.zeros((JP - I, S), F32)

    def g_block(rows):
        return (jnp.concatenate([rows[0], pad, rows[1], pad], axis=0) * (1.0 / S)).T.astype(BF16)

    for j, k in enumerate(direct):
        g1send[k] = g_block(g_rows(yh, k))
        g1send[NZ + j] = g_block(g_rows(1 - yh, k))

    def g_to(half, k, slot):
        q = (z + k) & (NZ - 1)
        for t in range(NS):
            send(g1send.at[slot, pl.ds(t * SB, SB)], grecv.at[slot * NS + s], 3, (r, half * NZ + q, t))

    for k in range(1, NS):
        t = (s + k) & (NS - 1)
        send(g1send.at[0, pl.ds(pl.multiple_of(t * SB, SB), SB)], grecv.at[s], 3, (r, c, t))
    grecv[s] = g1send[0, pl.ds(srow, SB), :]
    for k in direct[1:]:
        g_to(yh, k, k)

    for ah in range(2):
        for q in range((I * CH) // S):
            ltt[:, pl.ds((ah * I * CH) + q * S, S)] = ltf[ah, pl.ds(q * S, S), :].T.astype(BF16)

    def h_step(k):
        rhs = jnp.concatenate(
            [
                jnp.concatenate([dbuf[:, ah, 2 * k + q].reshape(I * CH, L2) for ah in range(2)], axis=0)
                for q in range(2)
            ],
            axis=1,
        )
        h = dot(ltt[...], rhs, NN).astype(BF16)
        hsend[2 * k] = h[:, :L2]
        hsend[2 * k + 1] = h[:, L2:]

    loop(0, NE // 2, h_step, 2)

    for t in range(NS // 2):
        send(hsend.at[:, pl.ds(pl.multiple_of((2 * t + 1 - core) * SB, SB), SB)], hx.at[t], 11, sibling)

    wait_recv(wrecv.at[pl.ds(0, NP - 1)], 4)
    total = wrecv[0].astype(F32)
    for q in range(1, NP):
        total = total + wrecv[q].astype(F32)
    w1send[...] = total.astype(BF16)
    loop(1, NZ, lambda k: send(w1send, zrecv.at[z], 6, z_peer(k)))
    zrecv[z] = w1send[...]
    wait_recv(hx, 11)
    for t in range(NS // 2):
        h1send[t] = (
            hsend[:, pl.ds(pl.multiple_of((2 * t + core) * SB, SB), SB), :].astype(F32) + hx[t].astype(F32)
        ).astype(BF16)
    own = r * (NS // 2) + (s >> 1)
    for k in range(1, NR):
        for t in range(NS // 2):
            q = (r + k) & (NR - 1)
            send(h1send.at[t, pl.ds(pl.multiple_of(q * NER, NER), NER)], hrecv.at[own], 5, (q, c, 2 * t + core))
    for k in range(1, NS // 2):
        t = ((s >> 1) + k) & (NS // 2 - 1)
        send(h1send.at[t, pl.ds(erow, NER)], hrecv.at[own], 5, (r, c, 2 * t + core))
    hrecv[own] = h1send[s >> 1, pl.ds(erow, NER)]

    for j, k in enumerate(direct):
        g_to(1 - yh, k, NZ + j)

    def p_step(k):
        rhs = jnp.concatenate(
            [obuf[2 * k].reshape(NE * C, L2), obuf[2 * k + 1].reshape(NE * C, L2)], axis=1
        )
        y = dot(w2t[...], rhs, NN)
        lo, hi = y[:CP], y[CP:]
        a = lo[:, :L2] + pltpu.roll(hi[:, :L2], JP, 1)
        b = hi[:, L2:] + pltpu.roll(lo[:, L2:], JP, 1)
        lane = lax.broadcasted_iota(jnp.int32, a.shape, 1)
        m = jnp.where(lane < JP, a, b).T * (1.0 / S) + bias[...]
        m = m.astype(BF16)
        pair[2 * k] = m[:J]
        pair[2 * k + 1] = m[JP:JP + J]

    loop(0, I // 4, p_step, 4)

    wait_recv(gx, 10)
    for j, k in enumerate(relayed):
        rows = g_rows(yh, k)
        g1send[k] = g_block([rows[h] + gx[j, pl.ds(h * I, I), :].astype(F32) for h in range(2)])
        g_to(yh, k, k)

    wait_recv(zrecv.at[pl.ds(0, NZ - 1)], 6)
    total = zrecv[0].astype(F32)
    for q in range(1, NZ):
        total = total + zrecv[q].astype(F32)
    w2send[...] = (total * (1.0 / S)).astype(BF16)
    loop(1, NP, lambda k: send(w2send, wall.at[ip], 7, plane_peer(k)))
    wall[ip] = w2send[...]

    loop(I // 4, I // 2, p_step, 4)

    wait_recv(hrecv.at[pl.ds(0, NA // 2 - 1)], 5)
    for e in range(NER):
        total = hrecv[0, e].astype(F32)
        for q in range(1, NA // 2):
            total = total + hrecv[q, e].astype(F32)
        total = total * (1.0 / S)
        for h in range(2):
            rg[:, 2 * e + h, :] = total[:, h * JP:h * JP + J]

    wait_recv(wall.at[pl.ds(0, NP - 1)], 7)
    for ah in range(2):
        for e in range(NE):
            x = wall[2 * e + ah].astype(F32)
            for h in range(2):
                wg[pl.ds(ah * CH * 2 * NE + 2 * e + h, CH, stride=2 * NE), :] = x[:, h * CP:(h + 1) * CP]

    wait_recv(grecv.at[pl.ds(0, NG * NS - 1)], 3)
    parts = []
    for q in range(NS):
        total = grecv[q].astype(F32)
        for t in range(1, NG):
            total = total + grecv[t * NS + q].astype(F32)
        parts.append(total)
    for h in range(2):
        lg[:, h, :] = jnp.concatenate([x[:, h * JP:h * JP + I] for x in parts], axis=1)

    wait_send(gtf.at[pl.ds(0, (NZ * NS - 1) * SB // 2)], 0)
    wait_send(rbuf.at[pl.ds(0, (NE * (NA // 2 - 1)) // NA)], 1)
    wait_send(rbuf.at[pl.ds(0, NE // 2)], 9)
    wait_send(lbuf.at[pl.ds(0, NZ)], 2)
    wait_send(grecv.at[pl.ds(0, NG * NS - 1)], 3)
    wait_send(gx, 10)
    wait_send(hx, 11)
    wait_send(wrecv.at[pl.ds(0, NP - 1)], 4)
    wait_send(hrecv.at[pl.ds(0, NA // 2 - 1)], 5)
    wait_send(zrecv.at[pl.ds(0, NZ - 1)], 6)
    wait_send(wall.at[pl.ds(0, NP - 1)], 7)


def finish(*refs):
    sem = refs[8]
    copies = [pltpu.make_async_copy(refs[q], refs[4 + q], sem.at[q]) for q in range(4)]
    for copy in copies:
        copy.start()
    for copy in copies:
        copy.wait()


def body(n, left, right, projection, bias, cotangent):
    NR, NC, NS, NZ = n
    NYH = NC // NZ
    NA = NR * NS
    NP = NR * NYH * NS
    SB = left.shape[0]
    S = SB * NS
    C = 2 * NC
    CH = C // 2
    I, J, CP = cotangent.shape
    JP = 64 if J == 48 else 2 * J
    L2 = 2 * JP
    NER = right.shape[1] // 2
    NE = NER * NR

    far = sum(min(k, NZ - k) > NZ // 4 for k in range(NZ))

    vmem = pl.BlockSpec(memory_space=pltpu.VMEM)
    hbm = pl.BlockSpec(memory_space=pl.ANY)
    scratch = [
        pltpu.VMEM((1, CP), F32),
        pltpu.VMEM(left.shape, BF16),
        pltpu.VMEM(right.shape, BF16),
        pltpu.VMEM((SB * 2 * NER, 128), F32),
        pltpu.VMEM(cotangent.shape, BF16),
        pltpu.VMEM(projection.shape, BF16),
        pltpu.VMEM(projection.shape, F32),
        pltpu.VMEM((NE * C, 2 * CP), BF16),
        pltpu.VMEM((2 * CP, NE * C), BF16),
        pltpu.VMEM((NS, SB, L2), BF16),
        pltpu.VMEM((NER, SB, L2), BF16),
        pltpu.VMEM((NC, S, L2), BF16),
        pltpu.VMEM((2, I * CH, S), F32),
        pltpu.VMEM((S, I * C), BF16),
        pltpu.VMEM((NE, S, L2), BF16),
        pltpu.VMEM((NE * L2, S), BF16),
        pltpu.VMEM((I, 2, NE, CH, L2), BF16),
        pltpu.VMEM((I, 2, NE, CH, L2), BF16),
        pltpu.VMEM((I, L2, 2 * CP), BF16),
        pltpu.VMEM((I * C, S), F32),
        pltpu.VMEM((far, 2 * I, S), BF16),
        pltpu.VMEM((far, 2 * I, S), BF16),
        pltpu.VMEM((2 * NZ - far, S, L2), BF16),
        pltpu.VMEM(((2 * NZ - far) * NS, SB, L2), BF16),
        pltpu.VMEM((NE, S, L2), BF16),
        pltpu.VMEM((NS // 2, NE, SB, L2), BF16),
        pltpu.VMEM((NS // 2, NE, SB, L2), BF16),
        pltpu.VMEM((NA // 2, NER, SB, L2), BF16),
        pltpu.VMEM((NP, CH, 2 * CP), BF16),
        pltpu.VMEM((NP, CH, 2 * CP), BF16),
        pltpu.VMEM((CH, 2 * CP), BF16),
        pltpu.VMEM((NZ, CH, 2 * CP), BF16),
        pltpu.VMEM((CH, 2 * CP), BF16),
        pltpu.VMEM((NP, CH, 2 * CP), BF16),
        pltpu.VMEM((NE * CH, 2 * CP), F32),
        pltpu.SemaphoreType.DMA((12,)),
        pltpu.SemaphoreType.DMA((12,)),
        pltpu.SemaphoreType.DMA((NZ,)),
        pltpu.SemaphoreType.DMA((NZ,)),
        pltpu.SemaphoreType.DMA((5,)),
    ]
    shapes = ((I, J, CP), BF16), (left.shape, F32), (right.shape, F32), (projection.shape, F32)
    results = pl.pallas_call(
        functools.partial(kernel, n),
        out_shape=tuple(pltpu.VMEM(shape, dtype) for shape, dtype in shapes),
        in_specs=[hbm] * 5,
        out_specs=(vmem,) * 4,
        scratch_shapes=scratch,
        compiler_params=pltpu.CompilerParams(
            collective_id=0, has_side_effects=True, vmem_limit_bytes=62 * 1024 * 1024
        ),
    )(left, right, cotangent, projection, bias.reshape(1, CP))
    return pl.pallas_call(
        finish,
        out_shape=tuple(jax.ShapeDtypeStruct(shape, dtype) for shape, dtype in shapes),
        in_specs=[vmem] * 4,
        out_specs=(hbm,) * 4,
        scratch_shapes=[pltpu.SemaphoreType.DMA((4,))],
        compiler_params=pltpu.CompilerParams(vmem_limit_bytes=4 * 1024 * 1024),
    )(*results)


def solution(mesh, nz=NZ):
    n = (mesh.shape["row"], mesh.shape["col"], mesh.shape["seq"], nz)
    return jax.shard_map(
        functools.partial(body, n),
        mesh=mesh,
        in_specs=(
            P("seq", "col", "row"),
            P("seq", "row", "col"),
            P(),
            P(),
            P(("row", "seq"), "col", None),
        ),
        out_specs=(
            P(("row", "seq"), "col", None),
            P("seq", "col", "row"),
            P("seq", "row", "col"),
            P(),
        ),
        check_vma=False,
    )
```

```python
import functools
import math

import jax
import jax.numpy as jnp
from jax import lax
from jax.experimental import pallas as pl
from jax.experimental.pallas import tpu as pltpu
from jax.sharding import PartitionSpec as P

MESH = pl.DeviceIdType.MESH
F32 = jnp.float32
BF16 = jnp.bfloat16
NZ = 8


def dot(a, b, dims):
    return lax.dot_general(a, b, (dims, ((), ())), preferred_element_type=F32)


def log2(size):
    return size.bit_length() - 1


NN = ((1,), (0,))
NT = ((1,), (1,))


def kernel(n, left, right, cot_in, w_in, bias_in, pair, lg, rg, wg,
           bias, leftv, rightv, rightf, cot, wv, wf, w3, w2t, xl, xr,
           lbuf, ltf, ltt, rbuf, rt, dbuf, obuf, cbd, gtf, gsend, gx, g1send, grecv, hsend, hx, h1send, hrecv,
           wsend, wrecv, w1send, zrecv, w2send, wall, wacc, ssem, rsem, nsem, fsem, lsem):
    NR, NC, NS, NZ = n
    NYH = NC // NZ
    NA = NR * NS
    NP = NR * NYH * NS
    SB = xl.shape[1]
    I, J, CP = cot.shape
    JP = xl.shape[2] // 2
    L2 = 2 * JP
    NER = xr.shape[0]
    NE = NER * NR
    C = 2 * NC
    CH = C // 2
    S = SB * NS
    IB = I

    r = lax.axis_index("row")
    c = lax.axis_index("col")
    s = lax.axis_index("seq")
    z = c & (NZ - 1)
    yh = c // NZ
    ia = r * NS + s
    ip = (r * NYH + yh) * NS + s

    def seq_peer(k):
        return (r, c, (s + k) & (NS - 1))

    def plane_device(t):
        return (t >> log2(NYH * NS), ((t >> log2(NS)) & (NYH - 1)) * NZ + z, t & (NS - 1))

    def plane_peer(k):
        return plane_device((ip + k) & (NP - 1))

    def z_peer(k):
        return (r, yh * NZ + ((z + k) & (NZ - 1)), s)

    def loop(lo, hi, f, unroll=1):
        unroll = math.gcd(hi - lo, unroll)

        def step(k, carry):
            for q in range(unroll):
                f(lo + k * unroll + q)
            return carry
        lax.fori_loop(0, (hi - lo) // unroll, step, 0)

    def send(src, dst, phase, dev):
        pltpu.make_async_remote_copy(
            src_ref=src, dst_ref=dst, send_sem=ssem.at[phase], recv_sem=rsem.at[phase],
            device_id=dev, device_id_type=MESH,
        ).start()

    def wait_recv(ref, phase):
        pltpu.make_async_copy(ref, ref, rsem.at[phase]).wait()

    def wait_send(ref, phase):
        pltpu.make_async_copy(ref, ref, ssem.at[phase]).wait()

    loads = [
        pltpu.make_async_copy(src, dst, lsem.at[q])
        for q, (src, dst) in enumerate([(left, leftv), (right, rightv), (w_in, wv), (cot_in, cot), (bias_in, bias)])
    ]
    for load in loads:
        load.start()

    barrier = pltpu.get_barrier_semaphore()

    def greet(dev):
        pl.semaphore_signal(barrier, inc=1, device_id=dev, device_id_type=MESH)

    near = sorted(range(NZ), key=lambda k: min(k, NZ - k))
    relayed = [k for k in near if min(k, NZ - k) > NZ // 4]
    direct = [k for k in near if k not in relayed]
    NG = NZ + len(direct)

    def greet_z(k):
        t = (z + k) & (NZ - 1)
        for q in range(NS):
            greet((r, yh * NZ + t, q))
        if k in direct:
            for q in range(NS):
                greet((r, (1 - yh) * NZ + t, q))

    def greet_row(k):
        for h in range(NYH):
            for t in range(NS):
                greet(((r + k) & (NR - 1), h * NZ + z, t))

    loop(1, NR, greet_row)
    for k in relayed[::-1] + direct[:0:-1]:
        greet_z(k)
    for k in range(1, NS):
        greet(seq_peer(k))
    for q in range(NS):
        greet((r, (1 - yh) * NZ + z, q))

    loads[0].wait()
    loads[1].wait()
    lf = leftv[...].astype(F32)
    zero = jnp.zeros((SB, JP - I), F32)
    for q in range(NS):
        parts = []
        for h in range(2):
            parts += [lf[:, h, q * I:(q + 1) * I], zero]
        xl[q] = jnp.concatenate(parts, axis=1).astype(BF16)
    rightf[:, pl.ds(0, J)] = rightv[...].astype(F32).reshape(SB * 2 * NER, J)
    for e in range(NER):
        parts = []
        for h in range(2):
            parts += [rightf[pl.ds(2 * e + h, SB, stride=2 * NER), :][:, :J], zero]
        xr[e] = jnp.concatenate(parts, axis=1).astype(BF16)

    srow = pl.multiple_of(s * SB, SB)
    erow = pl.multiple_of(r * NER, NER)

    pl.semaphore_wait(barrier, (NR - 1) * NYH * NS + (NZ - 1) * 2 * NS - len(relayed) * NS + 2 * NS - 1)

    def copy(src, dst, send_sem, recv_sem, dev):
        pltpu.make_async_remote_copy(
            src_ref=src, dst_ref=dst, send_sem=send_sem, recv_sem=recv_sem, device_id=dev, device_id_type=MESH
        ).start()

    core = s & 1
    sibling = (r, c, s + 1 - 2 * core)

    def right_to(dev):
        send(xr, rbuf.at[pl.ds(erow, NER), pl.ds(srow, SB)], 1, dev)

    for k in range(1, NR):
        for t in range(NS // 2):
            right_to(((r + k) & (NR - 1), c, 2 * t + core))
    for k in range(1, NS // 2):
        right_to((r, c, (s + 2 * k) & (NS - 1)))

    def left_to(half, k, send_sem, recv_sem):
        for t in range(NS):
            copy(xl.at[t], lbuf.at[c, pl.ds(srow, SB)], send_sem, recv_sem,
                 (r, half * NZ + ((z + k) & (NZ - 1)), t))

    arrival = relayed[::-1] + direct
    for k in arrival:
        if k == 0:
            for t in range(1, NS):
                copy(xl.at[(s + t) & (NS - 1)], lbuf.at[c, pl.ds(srow, SB)], ssem.at[0], nsem.at[0], seq_peer(t))
        else:
            left_to(yh, k, ssem.at[0], nsem.at[k])
    for k in direct:
        left_to(1 - yh, k, ssem.at[2], fsem.at[k])
    lbuf[c, pl.ds(srow, SB), :] = xl[s]
    rbuf[pl.ds(erow, NER), pl.ds(srow, SB), :] = xr[...]

    loads[2].wait()
    loads[3].wait()
    loads[4].wait()
    wf[...] = wv[...].astype(F32)
    for ah in range(2):
        for e in range(NE):
            for h in range(2):
                w3[pl.ds((ah * NE + e) * CH, CH), pl.ds(h * CP, CP)] = (
                    wf[pl.ds(ah * CH * 2 * NE + 2 * e + h, CH, stride=2 * NE), :].astype(BF16)
                )
    w2t[...] = w3[...].astype(F32).T.astype(BF16)

    def d_step(k):
        zc = jnp.zeros((JP, CP), BF16)
        for q in range(2):
            i = 2 * k + q
            a = jnp.concatenate([cot[i], jnp.zeros((JP - J, CP), BF16)], axis=0)
            cbd[i, pl.ds(0, JP), :] = jnp.concatenate([a, zc], axis=1)
            cbd[i, pl.ds(JP, JP), :] = jnp.concatenate([zc, a], axis=1)
        rhs = cbd[pl.ds(2 * k, 2)].reshape(2 * L2, 2 * CP)
        d = dot(w3[...], rhs, NT).astype(BF16)
        dbuf[2 * k] = d[:, :L2].reshape(2, NE, CH, L2)
        dbuf[2 * k + 1] = d[:, L2:].reshape(2, NE, CH, L2)

    loop(0, I // 2, d_step, 4)

    def rows_of(ah, q):
        x = lbuf[ah * NZ + q].astype(F32).T
        for h in range(2):
            ltf[ah, pl.ds(2 * q + h, I, stride=CH), :] = x[h * JP:h * JP + I]

    for k in arrival:
        q = (z + NZ - k) & (NZ - 1)
        block = lbuf.at[yh * NZ + q]
        got = lbuf.at[0, pl.ds(0, S - SB if k == 0 else S)]
        pltpu.make_async_copy(got, got, nsem.at[k]).wait()
        if k in relayed:
            copy(block, block, ssem.at[2], fsem.at[k], (r, (1 - yh) * NZ + z, s))
        rows_of(yh, q)
        if k == relayed[0]:
            wait_recv(rbuf.at[pl.ds(0, (NE * (NA // 2 - 1)) // NA)], 1)
            for t in range(NS // 2):
                part = rbuf.at[:, pl.ds(pl.multiple_of((2 * t + core) * SB, SB), SB)]
                send(part, part, 9, sibling)

    wait_recv(rbuf.at[pl.ds(0, NE // 2)], 9)

    def half_step(ah):
        lh = ltf.at[ah]

        def o_step(k):
            base = k * IB
            a = lh[pl.ds(pl.multiple_of(base * CH, IB * CH), IB * CH), :].astype(BF16)
            rhs = jnp.concatenate([rbuf[e] for e in range(NE)], axis=1)
            o = dot(a, rhs, NN).astype(BF16)
            for e in range(NE):
                obuf[pl.ds(base, IB), ah, e] = o[:, e * L2:(e + 1) * L2].reshape(IB, CH, L2)

        loop(0, I // IB, o_step)
        wacc[...] = jnp.zeros_like(wacc)

        def w_step(k):
            base = k * 8
            lhs = jnp.concatenate([obuf[base + q, ah].reshape(NE * CH, L2) for q in range(8)], axis=1)
            wacc[...] += dot(lhs, cbd[pl.ds(base, 8)].reshape(8 * L2, 2 * CP), NN)

        loop(0, I // 8, w_step, 3)
        for e in range(NE):
            wsend[2 * e + ah] = wacc[pl.ds(e * CH, CH), :].astype(BF16)

        def send_piece(k):
            t = 2 * (((ip >> 1) + k) & (NE - 1)) + ah

            @pl.when(t != ip)
            def _():
                send(wsend.at[t], wrecv.at[ip], 4, plane_device(t))

        loop(0, NE, send_piece)

    half_step(yh)

    for k in direct + relayed[::-1]:
        pltpu.make_async_copy(lbuf.at[0], lbuf.at[0], fsem.at[k]).wait()
        rows_of(1 - yh, (z + NZ - k) & (NZ - 1))
    half_step(1 - yh)
    wrecv[ip] = wsend[ip]

    for e in range(NE):
        rt[pl.ds(e * L2, L2), :] = rbuf[e].astype(F32).T.astype(BF16)

    def g_step(k):
        base = k * 8
        lhs = jnp.concatenate(
            [dbuf[pl.ds(base, 8), :, e].reshape(8 * C, L2) for e in range(NE)], axis=1
        )
        gtf[pl.ds(pl.multiple_of(base * C, 8 * C), 8 * C), :] = dot(lhs, rt[...], NN)

    loop(0, I // 8, g_step, 3)

    def g_rows(half, k):
        q = half * NZ + ((z + k) & (NZ - 1))
        return [gtf[pl.ds(2 * q + h, I, stride=C), :] for h in range(2)]

    for j, k in enumerate(relayed):
        gsend[j] = jnp.concatenate(g_rows(1 - yh, k), axis=0).astype(BF16)
    send(gsend, gx, 10, (r, (1 - yh) * NZ + z, s))

    pad = jnp.zeros((JP - I, S), F32)

    def g_block(rows):
        return (jnp.concatenate([rows[0], pad, rows[1], pad], axis=0) * (1.0 / S)).T.astype(BF16)

    for j, k in enumerate(direct):
        g1send[k] = g_block(g_rows(yh, k))
        g1send[NZ + j] = g_block(g_rows(1 - yh, k))

    def g_to(half, k, slot):
        q = (z + k) & (NZ - 1)
        for t in range(NS):
            send(g1send.at[slot, pl.ds(t * SB, SB)], grecv.at[slot * NS + s], 3, (r, half * NZ + q, t))

    for k in range(1, NS):
        t = (s + k) & (NS - 1)
        send(g1send.at[0, pl.ds(pl.multiple_of(t * SB, SB), SB)], grecv.at[s], 3, (r, c, t))
    grecv[s] = g1send[0, pl.ds(srow, SB), :]
    for k in direct[1:]:
        g_to(yh, k, k)

    for ah in range(2):
        for q in range((I * CH) // S):
            ltt[:, pl.ds((ah * I * CH) + q * S, S)] = ltf[ah, pl.ds(q * S, S), :].T.astype(BF16)

    def h_step(k):
        rhs = jnp.concatenate(
            [
                jnp.concatenate([dbuf[:, ah, 2 * k + q].reshape(I * CH, L2) for ah in range(2)], axis=0)
                for q in range(2)
            ],
            axis=1,
        )
        h = dot(ltt[...], rhs, NN).astype(BF16)
        hsend[2 * k] = h[:, :L2]
        hsend[2 * k + 1] = h[:, L2:]

    loop(0, NE // 2, h_step, 2)

    for t in range(NS // 2):
        send(hsend.at[:, pl.ds(pl.multiple_of((2 * t + 1 - core) * SB, SB), SB)], hx.at[t], 11, sibling)

    wait_recv(wrecv.at[pl.ds(0, NP - 1)], 4)
    total = wrecv[0].astype(F32)
    for q in range(1, NP):
        total = total + wrecv[q].astype(F32)
    w1send[...] = total.astype(BF16)
    loop(1, NZ, lambda k: send(w1send, zrecv.at[z], 6, z_peer(k)))
    zrecv[z] = w1send[...]
    wait_recv(hx, 11)
    for t in range(NS // 2):
        h1send[t] = (
            hsend[:, pl.ds(pl.multiple_of((2 * t + core) * SB, SB), SB), :].astype(F32) + hx[t].astype(F32)
        ).astype(BF16)
    own = r * (NS // 2) + (s >> 1)
    for k in range(1, NR):
        for t in range(NS // 2):
            q = (r + k) & (NR - 1)
            send(h1send.at[t, pl.ds(pl.multiple_of(q * NER, NER), NER)], hrecv.at[own], 5, (q, c, 2 * t + core))
    for k in range(1, NS // 2):
        t = ((s >> 1) + k) & (NS // 2 - 1)
        send(h1send.at[t, pl.ds(erow, NER)], hrecv.at[own], 5, (r, c, 2 * t + core))
    hrecv[own] = h1send[s >> 1, pl.ds(erow, NER)]

    for j, k in enumerate(direct):
        g_to(1 - yh, k, NZ + j)

    def p_step(k):
        rhs = jnp.concatenate(
            [obuf[2 * k].reshape(NE * C, L2), obuf[2 * k + 1].reshape(NE * C, L2)], axis=1
        )
        y = dot(w2t[...], rhs, NN)
        lo, hi = y[:CP], y[CP:]
        a = lo[:, :L2] + pltpu.roll(hi[:, :L2], JP, 1)
        b = hi[:, L2:] + pltpu.roll(lo[:, L2:], JP, 1)
        lane = lax.broadcasted_iota(jnp.int32, a.shape, 1)
        m = jnp.where(lane < JP, a, b).T * (1.0 / S) + bias[...]
        m = m.astype(BF16)
        pair[2 * k] = m[:J]
        pair[2 * k + 1] = m[JP:JP + J]

    loop(0, I // 4, p_step, 4)

    wait_recv(gx, 10)
    for j, k in enumerate(relayed):
        rows = g_rows(yh, k)
        g1send[k] = g_block([rows[h] + gx[j, pl.ds(h * I, I), :].astype(F32) for h in range(2)])
        g_to(yh, k, k)

    wait_recv(zrecv.at[pl.ds(0, NZ - 1)], 6)
    total = zrecv[0].astype(F32)
    for q in range(1, NZ):
        total = total + zrecv[q].astype(F32)
    w2send[...] = (total * (1.0 / S)).astype(BF16)
    loop(1, NP, lambda k: send(w2send, wall.at[ip], 7, plane_peer(k)))
    wall[ip] = w2send[...]

    loop(I // 4, I // 2, p_step, 4)

    wait_recv(hrecv.at[pl.ds(0, NA // 2 - 1)], 5)
    for e in range(NER):
        total = hrecv[0, e].astype(F32)
        for q in range(1, NA // 2):
            total = total + hrecv[q, e].astype(F32)
        total = total * (1.0 / S)
        for h in range(2):
            rg[:, 2 * e + h, :] = total[:, h * JP:h * JP + J]

    wait_recv(wall.at[pl.ds(0, NP - 1)], 7)
    for ah in range(2):
        for e in range(NE):
            x = wall[2 * e + ah].astype(F32)
            for h in range(2):
                wg[pl.ds(ah * CH * 2 * NE + 2 * e + h, CH, stride=2 * NE), :] = x[:, h * CP:(h + 1) * CP]

    wait_recv(grecv.at[pl.ds(0, NG * NS - 1)], 3)
    parts = []
    for q in range(NS):
        total = grecv[q].astype(F32)
        for t in range(1, NG):
            total = total + grecv[t * NS + q].astype(F32)
        parts.append(total)
    for h in range(2):
        lg[:, h, :] = jnp.concatenate([x[:, h * JP:h * JP + I] for x in parts], axis=1)

    wait_send(gtf.at[pl.ds(0, (NZ * NS - 1) * SB // 2)], 0)
    wait_send(rbuf.at[pl.ds(0, (NE * (NA // 2 - 1)) // NA)], 1)
    wait_send(rbuf.at[pl.ds(0, NE // 2)], 9)
    wait_send(lbuf.at[pl.ds(0, NZ)], 2)
    wait_send(grecv.at[pl.ds(0, NG * NS - 1)], 3)
    wait_send(gx, 10)
    wait_send(hx, 11)
    wait_send(wrecv.at[pl.ds(0, NP - 1)], 4)
    wait_send(hrecv.at[pl.ds(0, NA // 2 - 1)], 5)
    wait_send(zrecv.at[pl.ds(0, NZ - 1)], 6)
    wait_send(wall.at[pl.ds(0, NP - 1)], 7)


def finish(*refs):
    sem = refs[8]
    copies = [pltpu.make_async_copy(refs[q], refs[4 + q], sem.at[q]) for q in range(4)]
    for copy in copies:
        copy.start()
    for copy in copies:
        copy.wait()


def body(n, left, right, projection, bias, cotangent):
    NR, NC, NS, NZ = n
    NYH = NC // NZ
    NA = NR * NS
    NP = NR * NYH * NS
    SB = left.shape[0]
    S = SB * NS
    C = 2 * NC
    CH = C // 2
    I, J, CP = cotangent.shape
    JP = 64 if J == 48 else 2 * J
    L2 = 2 * JP
    NER = right.shape[1] // 2
    NE = NER * NR

    far = sum(min(k, NZ - k) > NZ // 4 for k in range(NZ))

    vmem = pl.BlockSpec(memory_space=pltpu.VMEM)
    hbm = pl.BlockSpec(memory_space=pl.ANY)
    scratch = [
        pltpu.VMEM((1, CP), F32),
        pltpu.VMEM(left.shape, BF16),
        pltpu.VMEM(right.shape, BF16),
        pltpu.VMEM((SB * 2 * NER, 128), F32),
        pltpu.VMEM(cotangent.shape, BF16),
        pltpu.VMEM(projection.shape, BF16),
        pltpu.VMEM(projection.shape, F32),
        pltpu.VMEM((NE * C, 2 * CP), BF16),
        pltpu.VMEM((2 * CP, NE * C), BF16),
        pltpu.VMEM((NS, SB, L2), BF16),
        pltpu.VMEM((NER, SB, L2), BF16),
        pltpu.VMEM((NC, S, L2), BF16),
        pltpu.VMEM((2, I * CH + CH, S), F32),
        pltpu.VMEM((S, I * C), BF16),
        pltpu.VMEM((NE, S, L2), BF16),
        pltpu.VMEM((NE * L2, S), BF16),
        pltpu.VMEM((I, 2, NE, CH, L2), BF16),
        pltpu.VMEM((I, 2, NE, CH, L2), BF16),
        pltpu.VMEM((I, L2, 2 * CP), BF16),
        pltpu.VMEM((I * C + C, S), F32),
        pltpu.VMEM((far, 2 * I, S), BF16),
        pltpu.VMEM((far, 2 * I, S), BF16),
        pltpu.VMEM((2 * NZ - far, S, L2), BF16),
        pltpu.VMEM(((2 * NZ - far) * NS, SB, L2), BF16),
        pltpu.VMEM((NE, S, L2), BF16),
        pltpu.VMEM((NS // 2, NE, SB, L2), BF16),
        pltpu.VMEM((NS // 2, NE, SB, L2), BF16),
        pltpu.VMEM((NA // 2, NER, SB, L2), BF16),
        pltpu.VMEM((NP, CH, 2 * CP), BF16),
        pltpu.VMEM((NP, CH, 2 * CP), BF16),
        pltpu.VMEM((CH, 2 * CP), BF16),
        pltpu.VMEM((NZ, CH, 2 * CP), BF16),
        pltpu.VMEM((CH, 2 * CP), BF16),
        pltpu.VMEM((NP, CH, 2 * CP), BF16),
        pltpu.VMEM((NE * CH, 2 * CP), F32),
        pltpu.SemaphoreType.DMA((12,)),
        pltpu.SemaphoreType.DMA((12,)),
        pltpu.SemaphoreType.DMA((NZ,)),
        pltpu.SemaphoreType.DMA((NZ,)),
        pltpu.SemaphoreType.DMA((5,)),
    ]
    shapes = ((I, J, CP), BF16), (left.shape, F32), (right.shape, F32), (projection.shape, F32)
    results = pl.pallas_call(
        functools.partial(kernel, n),
        out_shape=tuple(pltpu.VMEM(shape, dtype) for shape, dtype in shapes),
        in_specs=[hbm] * 5,
        out_specs=(vmem,) * 4,
        scratch_shapes=scratch,
        compiler_params=pltpu.CompilerParams(
            collective_id=0, has_side_effects=True, vmem_limit_bytes=62 * 1024 * 1024
        ),
    )(left, right, cotangent, projection, bias.reshape(1, CP))
    return pl.pallas_call(
        finish,
        out_shape=tuple(jax.ShapeDtypeStruct(shape, dtype) for shape, dtype in shapes),
        in_specs=[vmem] * 4,
        out_specs=(hbm,) * 4,
        scratch_shapes=[pltpu.SemaphoreType.DMA((4,))],
        compiler_params=pltpu.CompilerParams(vmem_limit_bytes=4 * 1024 * 1024),
    )(*results)


def solution(mesh, nz=NZ):
    n = (mesh.shape["row"], mesh.shape["col"], mesh.shape["seq"], nz)
    return jax.shard_map(
        functools.partial(body, n),
        mesh=mesh,
        in_specs=(
            P("seq", "col", "row"),
            P("seq", "row", "col"),
            P(),
            P(),
            P(("row", "seq"), "col", None),
        ),
        out_specs=(
            P(("row", "seq"), "col", None),
            P("seq", "col", "row"),
            P("seq", "row", "col"),
            P(),
        ),
        check_vma=False,
    )
```
